128 devices in a mesh: sec: 4 (over x_lo, core), swath: 32 (over y, z, x_hi).
Axes of the slice: x: 4 (x_hi: 2, x_lo: 2; x = x_hi * 2 + x_lo), y: 4, z: 4, core: 2. Of those that a mesh axis runs over, the one named last changes fastest.
Arguments:
- radar_l: bfloat16 [6, 1536, 4096], P(None, 'sec', 'swath'), may hold values from -6 to 6
- radar_s: bfloat16 [6, 1024, 4096], P(None, 'sec', 'swath'), may hold values from -6 to 6
- weights_l: bfloat16 [49152, 128, 128], P(('sec', 'swath')), may hold values from -0.5 to 0.5
- weights_s: bfloat16 [32768, 128, 128], P(('sec', 'swath')), may hold values from -0.5 to 0.5
- owner_l: int32 [49152, 1], P(('sec', 'swath')), may hold values from 0 to 127; in each aligned block of 384 rows (0 to 383, 384 to 767, ...) at most 6 rows name the same one
- owner_s: int32 [32768, 1], P(('sec', 'swath')), may hold values from 0 to 127; in each aligned block of 256 rows (0 to 255, 256 to 511, ...) at most 4 rows name the same one
- slot_l: int32 [49152], P(('sec', 'swath')), may hold values from 0 to 255
- slot_s: int32 [32768], P(('sec', 'swath')), may hold values from 0 to 255
- models: float32 [16, 36], replicated, may hold values from -1 to 1
Outputs:
- fit: float32 [16, 1024, 4096], P(None, 'sec', 'swath')
The draws below stay inside these ranges and needn't reach their ends.
Inputs may be any that keep to these rules, and one draw needn't show every extreme that they name: `owner_l`: within the tiles of one device, each owner is named by at most 6 tiles. `owner_s`: within the tiles of one device, each owner is named by at most 4 tiles.
All inputs are finite; a program needn't handle non-finite values.
Results may differ from the reference program's by a relative error of at most 0.0038.
Values may be sent and summed in bfloat16 or wider, within the bound.
A program may use at most 192 MiB of HBM per device.

```python
import math
import jax
import jax.numpy as jnp
import numpy as np
from jax import lax

PIX = 128
TL_DEV = 384
TS_DEV = 256
NMODEL = 16
FIT_ITERS = 4
CAP_L = 6
CAP_S = 4
LINES_L = 1536
LINES_S = 1024
COLS = 4096
TILES_L = 49152
TILES_S = 32768
N_SEC = 4
N_SWATH = 32
DEVICES = 128


def place_ends(entries, key, low, largest):
    place = [jax.random.randint(jax.random.fold_in(key, axis), (), 0, length) for axis, length in enumerate(entries.shape)]
    longest = entries.shape.index(max(entries.shape))
    beside = place[:longest] + [(place[longest] + 1) % entries.shape[longest]] + place[longest + 1:]
    return entries.at[tuple(place)].set(low).at[tuple(beside)].set(largest)


def block_levels(rng, dims, split, least, top_value):
    level = 1.0
    for dim, blocks in split:
        steps = jax.random.uniform(jax.random.fold_in(jax.random.fold_in(rng, 6), dim), (blocks,), jnp.float32, least / len(split), top_value / len(split))
        level = level * jnp.repeat(jnp.exp(steps), dims[dim] // blocks).reshape((-1,) + (1,) * (len(dims) - 1 - dim))
    return level


def deal_out(stream_key, own, number, rows, count, top, most, skew):
    order = jax.random.permutation(stream_key, count)
    packed, usual = shares(count, rows * top, most, skew, True), shares(count, rows * top, most, skew, False)
    places = jnp.arange(count)

    def named(lengths, offset_by):
        used = int((lengths > 0).sum())
        fixed = max(1, used // 4)
        shifted = fixed + (places - fixed + offset_by * (used - fixed)) % max(1, count - fixed)
        return jnp.zeros((count,), jnp.int32).at[order[jnp.where(places < fixed, places, shifted)]].set(jnp.asarray(lengths, jnp.int32))

    lengths = jnp.where(number % 4 == 0, named(packed, number // 4), named(usual, number - number // 4 - 1))
    mixed = jax.random.permutation(jax.random.fold_in(own, 3), count)
    donor, sink = mixed[0:count // 2 * 2:2], mixed[1:count // 2 * 2:2]
    slack = jnp.minimum(lengths[donor] - 1, most - lengths[sink]) // 2
    slack = jnp.where((donor == order[0]) | (sink == order[0]) | (lengths[sink] == 0), 0, jnp.maximum(slack, 0))
    shifted = jax.random.randint(jax.random.fold_in(own, 4), (count // 2,), 0, 1 << 20) % (slack + 1)
    lengths = lengths.at[donor].add(-shifted).at[sink].add(shifted)
    members = jnp.searchsorted(jnp.cumsum(lengths), jnp.arange(rows * top), side="right").astype(jnp.int32)
    table = members.reshape(top, rows).T
    table = table[jax.random.permutation(jax.random.fold_in(own, 1), rows)]
    offset_by = jax.random.randint(jax.random.fold_in(own, 2), (rows, 1), 0, top)
    return jnp.take_along_axis(table, (jnp.arange(top)[None, :] + offset_by) % top, axis=1)


def shares(number_of, total, reach, skew, full):
    portions = [(1 << 20) // math.isqrt(grade ** skew) + 1 for grade in range(1, number_of + 1)]
    largest = reach if full else min(reach, max(-(-total // number_of), total * portions[0] // sum(portions)))
    least = 1 if total - largest >= number_of - 1 else 0
    holding, surplus = [largest] + [least] * (number_of - 1), total - largest - least * (number_of - 1)
    while surplus > 0:
        free = [i for i in range(1, number_of) if holding[i] < largest] or [i for i in range(1, number_of) if holding[i] < reach]
        mass, remaining = sum([portions[i] for i in free]), surplus
        for i in free:
            more = min(reach - holding[i], max(1, remaining * portions[i] // mass), surplus)
            holding[i] = holding[i] + more
            surplus = surplus - more
    return np.array(holding)


def gaussian(rng, shape, width, bound, shards=(), dtype=jnp.bfloat16):
    values = width * jax.random.normal(rng, shape, jnp.float32)
    if shards:
        values = values * block_levels(rng, shape, shards, -0.22, 0.18)
    return jnp.clip(values, -bound, bound).astype(dtype)


def setup_inputs(seed: int = 0) -> dict:
    arg_keys = jax.random.split(jax.random.key(seed), 10)
    radar_l = gaussian(arg_keys[0], (6, LINES_L, COLS), 1.0, 6.0, ((1, 4), (2, 32)))
    radar_s = gaussian(arg_keys[1], (6, LINES_S, COLS), 1.0, 6.0, ((1, 4), (2, 32)))
    weights_l = gaussian(arg_keys[2], (TILES_L, PIX, PIX), PIX ** -0.5, 0.5, ((0, 128),))
    weights_s = gaussian(arg_keys[3], (TILES_S, PIX, PIX), PIX ** -0.5, 0.5, ((0, 128),))
    owner_l_keys = jax.random.split(jax.random.fold_in(arg_keys[4], 1), TILES_L // TL_DEV)
    owner_l_turns = jax.random.permutation(jax.random.fold_in(arg_keys[4], 3), TILES_L // TL_DEV)
    owner_l = jax.vmap(lambda own, number: deal_out(jax.random.fold_in(arg_keys[4], 2), own, number, TL_DEV, DEVICES, 1, CAP_L, 2))(owner_l_keys, owner_l_turns).reshape((TILES_L, 1))
    owner_s_keys = jax.random.split(jax.random.fold_in(arg_keys[5], 1), TILES_S // TS_DEV)
    owner_s_turns = jax.random.permutation(jax.random.fold_in(arg_keys[5], 3), TILES_S // TS_DEV)
    owner_s = jax.vmap(lambda own, number: deal_out(jax.random.fold_in(arg_keys[5], 2), own, number, TS_DEV, DEVICES, 1, CAP_S, 2))(owner_s_keys, owner_s_turns).reshape((TILES_S, 1))
    slot_l = place_ends(jax.random.randint(arg_keys[6], (TILES_L,), 0, TS_DEV), jax.random.fold_in(arg_keys[6], 1), 0, TS_DEV - 1).astype(jnp.int32)
    slot_s = place_ends(jax.random.randint(arg_keys[7], (TILES_S,), 0, TS_DEV), jax.random.fold_in(arg_keys[7], 1), 0, TS_DEV - 1).astype(jnp.int32)
    models = gaussian(arg_keys[8], (NMODEL, 36), 36 ** -0.5, 1.0, (), jnp.float32)
    return dict(radar_l=radar_l, radar_s=radar_s, weights_l=weights_l, weights_s=weights_s, owner_l=owner_l, owner_s=owner_s, slot_l=slot_l, slot_s=slot_s, models=models)


cu_square = 0.25
fit_rate = 0.25
upper_pairs = [(first, second) for first in range(6) for second in range(first, 6)]
strict_pairs = [(first, second) for first in range(6) for second in range(first + 1, 6)]


def window_sum(padded):
    height = padded.shape[-2] - 2
    breadth = padded.shape[-1] - 2
    total = padded[..., 0:height, 0:breadth]
    for row_off in range(3):
        for col_off in range(3):
            if row_off + col_off > 0:
                total = total + padded[..., row_off:row_off + height, col_off:col_off + breadth]
    return total


def kuan_filter(padded):
    vectors = padded.astype(jnp.float32)
    height = vectors.shape[1] - 2
    breadth = vectors.shape[2] - 2
    local_mean = window_sum(vectors) / 9.0
    power = jnp.sum(vectors * vectors, axis=0)
    mean_power = window_sum(power) / 9.0
    spread = jnp.zeros_like(mean_power)
    for row_off in range(3):
        for col_off in range(3):
            spread = spread + (power[row_off:row_off + height, col_off:col_off + breadth] - mean_power) ** 2
    spread = spread / 9.0
    kuan_gain = spread / (spread + cu_square * mean_power * mean_power + 1.0)
    centre = vectors[:, 1:-1, 1:-1]
    return (local_mean + kuan_gain * (centre - local_mean)).astype(jnp.bfloat16)


def coherency(band_l, band_s):
    real_part = jnp.concatenate([band_l[0:3], band_s[0:3]], axis=0)
    imag_part = jnp.concatenate([band_l[3:6], band_s[3:6]], axis=0)
    parts = [real_part[first] * real_part[second] + imag_part[first] * imag_part[second] for first, second in upper_pairs]
    parts = parts + [imag_part[first] * real_part[second] - real_part[first] * imag_part[second] for first, second in strict_pairs]
    return jnp.stack(parts, axis=0)


def model_fit(smooth, models):
    powers = jnp.zeros((models.shape[0],) + smooth.shape[1:], jnp.float32)
    for iteration in range(FIT_ITERS):
        predicted = jnp.einsum('kc,klm->clm', models, powers, precision=lax.Precision.HIGHEST)
        powers = powers + fit_rate * jnp.einsum('kc,clm->klm', models, smooth - predicted, precision=lax.Precision.HIGHEST)
    return powers


def band_map(radar, weights, owner, slot, per_device):
    padded = jnp.pad(radar, ((0, 0), (1, 1), (1, 1)))
    filtered = kuan_filter(padded)
    device_total = N_SEC * N_SWATH
    tiles = filtered.reshape(6, N_SEC, per_device, N_SWATH, PIX).transpose(1, 3, 2, 0, 4).reshape(device_total, per_device, 6, PIX)
    weight_blocks = weights.reshape(device_total, per_device, PIX, PIX)

    def one_device(pair):
        weight_block, vector_block = pair
        return jnp.einsum('tqp,tcp->tcq', weight_block.astype(jnp.float32), vector_block.astype(jnp.float32)).astype(jnp.bfloat16)

    contribution = lax.map(one_device, (weight_blocks, tiles))
    flat_terms = contribution.reshape(device_total * per_device, 6 * PIX).astype(jnp.float32)
    segment = owner[:, 0].astype(jnp.int32) * TS_DEV + slot.astype(jnp.int32)
    summed = jax.ops.segment_sum(flat_terms, segment, num_segments=device_total * TS_DEV)
    return summed.reshape(N_SEC, N_SWATH, TS_DEV, 6, PIX).transpose(3, 0, 2, 1, 4).reshape(6, N_SEC * TS_DEV, N_SWATH * PIX)


def reference(radar_l, radar_s, weights_l, weights_s, owner_l, owner_s, slot_l, slot_s, models):
    map_l = band_map(radar_l, weights_l, owner_l, slot_l, TL_DEV)
    map_s = band_map(radar_s, weights_s, owner_s, slot_s, TS_DEV)
    joint = coherency(map_l, map_s)
    smooth = window_sum(jnp.pad(joint, ((0, 0), (1, 1), (1, 1)))) / 9.0
    return model_fit(smooth, models)
```

```python
import functools

import jax
import jax.numpy as jnp
from jax import lax
from jax.experimental import pallas as pl
from jax.experimental.pallas import tpu as pltpu
from jax.sharding import PartitionSpec as P

MESH = pl.DeviceIdType.MESH
F32, BF16, I32 = jnp.float32, jnp.bfloat16, jnp.int32
FIT_ITERS = 4
FIT_RATE = 0.25
N_SEC, N_SWATH, DEVICES = 4, 32, 128
LL, LS = 384, 256
CAP_L, CAP_S = 6, 4
CAP = CAP_L + CAP_S
TILES = LL + LS
ROWS = 64
MARK_ROW = 30
TOP_L, TOP_S = 8, 8 + LL + 16
EXT = LL + LS + 32
upper_pairs = [(i, j) for i in range(6) for j in range(i, 6)]
strict_pairs = [(i, j) for i in range(6) for j in range(i + 1, 6)]
NJ = len(upper_pairs) + len(strict_pairs)
AROUND = [(0, -1), (0, 1), (-1, -1), (-1, 1), (1, -1), (1, 1)]


def iota(shape, dim):
    return lax.broadcasted_iota(I32, shape, dim)


def dot(a, b, dims=((1,), (0,)), precision=None):
    return lax.dot_general(a, b, (dims, ((), ())), precision=precision, preferred_element_type=F32)


NT = ((1,), (1,))


def flag(cond):
    return jnp.where(cond, 1.0, 0.0).astype(F32)


def plan_kernel(owner_l, owner_s, slot_l, slot_s, models, source_ref, marks_ref, fit_ref):
    rows = []
    marks = []
    for owner, slot, lines, cap, first in ((owner_l, slot_l, LL, CAP_L, 0), (owner_s, slot_s, LS, CAP_S, LL)):
        hit = owner[...] == iota((lines, DEVICES), 1)
        hit_f = jnp.where(hit, 1.0, 0.0).astype(F32)
        lower = jnp.where(iota((lines, lines), 1) < iota((lines, lines), 0), 1.0, 0.0).astype(BF16)
        before = dot(lower, hit_f.astype(BF16))
        tile = iota((1, lines), 1) + first
        facts = jnp.concatenate(
            [
                slot[...].astype(F32),
                lax.rem(tile, 128).astype(F32),
                lax.div(tile, 128).astype(F32),
                jnp.ones((1, lines), F32),
                jnp.zeros((4, lines), F32),
            ],
            axis=0,
        ).astype(BF16)
        for k in range(cap):
            chosen = jnp.where(before == k, hit_f, 0.0).astype(BF16)
            got = dot(facts, chosen)
            filled = got[3:4]
            rows.append(got[1:2] + 128.0 * got[2:3] + (1.0 - filled) * TILES)
            marks.append(got[0:1] + filled - 1.0)
    pad = [jnp.zeros((16 - CAP, DEVICES), F32)]
    source_ref[...] = jnp.concatenate(rows + pad, axis=0).astype(I32)
    table = jnp.concatenate(marks + [jnp.zeros((DEVICES - CAP, DEVICES), F32)], axis=0)
    lane = lax.rem(iota((DEVICES, 128), 1), 32)
    spread = jnp.where((lax.rem(lane, CAP) == iota((DEVICES, 128), 0)) & (lane < 3 * CAP), 1.0, 0.0).astype(BF16)
    marks_ref[...] = dot(table.T.astype(BF16), spread) - jnp.where(lane < 3 * CAP, 0.0, 1.0)
    high = lax.Precision.HIGHEST
    m = models[...]
    gram = dot(m, m, NT, precision=high)
    total = m
    for _ in range(FIT_ITERS - 1):
        total = m + total - FIT_RATE * dot(gram, total, precision=high)
    total = total * (FIT_RATE / 9.0)
    left = jnp.where(lax.div(iota((128, 16), 0), 8) == iota((128, 16), 1), 1.0, 0.0).astype(F32)
    right = jnp.where(lax.div(iota((NJ, NJ * 8), 1), 8) == iota((NJ, NJ * 8), 0), 1.0, 0.0).astype(F32)
    wide = dot(dot(left, total, precision=high), right, precision=high)
    same = lax.rem(iota((128, NJ * 8), 0), 8) == lax.rem(iota((128, NJ * 8), 1), 8)
    wide = jnp.where(same, wide, 0.0)
    big = wide.astype(BF16)
    fit_ref[0:128] = big
    fit_ref[128:256] = (wide - big.astype(F32)).astype(BF16)


def main_kernel(
    radar_l, radar_s, weights_l, weights_s, source, marks,
    map_ref, cols_ref, rows_ref,
    wbuf, xbuf, pbuf, fbuf, vbuf, stage, payload, recv, maskbuf, edge, hcols, hrows, zedge, zrows,
    w_sem, hs_sem, hr_sem, send_sem, recv_sem, es_sem, er_sem,
):
    sec, swath = lax.axis_index("sec"), lax.axis_index("swath")
    me = sec * N_SWATH + swath

    w_copies = []
    for n, (src, first, count) in enumerate(((weights_l, 0, LL), (weights_s, LL, LS))):
        for part in range(4):
            size = count // 4
            w_copies.append(
                pltpu.make_async_copy(
                    src.at[pl.ds(part * size, size)],
                    wbuf.at[pl.ds(first + part * size, size)],
                    w_sem.at[4 * n + part],
                )
            )
    for copy in w_copies:
        copy.start()

    barrier = pltpu.get_barrier_semaphore()

    def greet(i, _):
        peer = lax.rem(me + i, DEVICES)
        pl.semaphore_signal(
            barrier, inc=1, device_id=(lax.div(peer, N_SWATH), lax.rem(peer, N_SWATH)), device_id_type=MESH
        )
        return 0

    lax.fori_loop(1, DEVICES, greet, 0)

    column, row = iota((16, 128), 1), iota((16, 128), 0)
    for radar, first, lines in ((radar_l, 0, LL), (radar_s, LL, LS)):
        total = jnp.zeros((16, lines), F32)
        for c in range(6):
            pick = jnp.where(
                ((row == c) & (column == 0)) | ((row == 8 + c) & (column == 127)), 1.0, 0.0
            ).astype(BF16)
            total = total + dot(pick, radar[c], NT)
        edge[:, first : first + lines] = total.astype(BF16)

    pl.semaphore_wait(barrier, DEVICES - 1)

    def beside(ds, dw):
        return (lax.rem(sec + ds + N_SEC, N_SEC), lax.rem(swath + dw + N_SWATH, N_SWATH))

    def around(src, slots, ssem, rsem):
        copies = []
        for n, (ds, dw) in enumerate(AROUND):
            copies.append(
                pltpu.make_async_remote_copy(
                    src_ref=src, dst_ref=slots.at[n], send_sem=ssem.at[n], recv_sem=rsem.at[n],
                    device_id=beside(-ds, -dw), device_id_type=MESH,
                )
            )
        return copies

    halo = around(edge, hcols, hs_sem, hr_sem)
    n = len(AROUND)
    for radar, first, lines in ((radar_l, 0, LL), (radar_s, 6, LS)):
        for side, (start, ds) in enumerate(((lines - 16, 1), (0, -1))):
            halo.append(
                pltpu.make_async_remote_copy(
                    src_ref=radar.at[:, pl.ds(start, 16), :],
                    dst_ref=hrows.at[side, pl.ds(first, 6)],
                    send_sem=hs_sem.at[n], recv_sem=hr_sem.at[n],
                    device_id=beside(ds, 0), device_id_type=MESH,
                )
            )
            n += 1
    for copy in halo:
        copy.start()

    for radar, top, lines in ((radar_l, TOP_L, LL), (radar_s, TOP_S, LS)):
        for c in range(6):
            xbuf[c, top : top + lines, :] = radar[c].astype(F32)
    fbuf[TILES] = jnp.zeros((8, 128), F32)
    fflat = fbuf.reshape((TILES + 1) * 8, 128)
    vbuf[...] = jnp.zeros((256, 128), F32)
    map_ref[...] = jnp.zeros((2, LS, 768), F32)
    r32 = lax.rem(iota((256, 128), 0), 32)
    for band in range(2):
        for c in range(3):
            k = r32 - 10 * c
            keep = (k >= 0) & (k < CAP_L) if band == 0 else (k >= CAP_L) & (k < CAP)
            maskbuf[band * 3 + c] = jnp.where(keep, 1.0, 0.0).astype(BF16)

    for copy in halo:
        copy.wait()

    has_up, has_down = flag(sec > 0), flag(sec < N_SEC - 1)
    has_left, has_right = flag(swath > 0), flag(swath < N_SWATH - 1)
    side = jnp.where(iota((16, TILES), 0) < 8, has_right, has_left)
    low = iota((16, TILES), 0) < 8

    def pick_sides(left_n, right_n):
        return jnp.where(low, hcols[right_n].astype(F32), hcols[left_n].astype(F32)) * side

    middle = pick_sides(0, 1)
    up, down = pick_sides(2, 3) * has_up, pick_sides(4, 5) * has_down
    corner_lane = iota((16, 128), 1)
    corners = jnp.where(corner_lane == 0, up[:, LL - 1 : LL], 0.0)
    corners = jnp.where(corner_lane == 1, down[:, 0:1], corners)
    corners = jnp.where(corner_lane == 2, up[:, TILES - 1 : TILES], corners)
    corners = jnp.where(corner_lane == 3, down[:, LL : LL + 1], corners)
    lines_of = jnp.concatenate([middle, corners], axis=1)
    lines_of = jnp.concatenate([lines_of, jnp.zeros((112, TILES + 128), F32)], axis=0).T.astype(BF16)
    pr, pc = iota((128, 128), 0), iota((128, 128), 1)
    for c in range(6):
        place = jnp.where(((pr == 8 + c) & (pc == 0)) | ((pr == c) & (pc == 127)), 1.0, 0.0).astype(BF16)
        placed = dot(lines_of, place)
        pbuf[c, TOP_L : TOP_L + LL, :] = placed[0:LL]
        pbuf[c, TOP_S : TOP_S + LS, :] = placed[LL:TILES]
        pbuf[c, TOP_L - 1 : TOP_L, :] = placed[TILES : TILES + 1]
        pbuf[c, TOP_L + LL : TOP_L + LL + 1, :] = placed[TILES + 1 : TILES + 2]
        pbuf[c, TOP_S - 1 : TOP_S, :] = placed[TILES + 2 : TILES + 3]
        pbuf[c, TOP_S + LS : TOP_S + LS + 1, :] = placed[TILES + 3 : TILES + 4]
        for top, lines, first in ((TOP_L, LL, 0), (TOP_S, LS, 6)):
            xbuf[c, top - 1 : top, :] = hrows[0, first + c].astype(F32)[15:16] * has_up
            xbuf[c, top + lines : top + lines + 1, :] = hrows[1, first + c].astype(F32)[0:1] * has_down

    lane80 = iota((80, 128), 1)

    def beside_lanes(x, p):
        return (
            jnp.where(lane80 == 0, p, pltpu.roll(x, 1, 1)),
            jnp.where(lane80 == 127, p, pltpu.roll(x, 127, 1)),
        )

    def lines_three(h):
        return (pltpu.roll(h, 1, 0)[8:72], h[8:72], pltpu.roll(h, 79, 0)[8:72])

    def filter_chunk(i, _):
        base = pl.multiple_of(i * 64 + jnp.where(i >= LL // 64, 16, 0), 8)
        tile = i * 64
        power = jnp.zeros((80, 128), F32)
        placed_power = jnp.zeros((80, 128), F32)
        for c in range(6):
            x, p = xbuf[c, pl.ds(base, 80), :], pbuf[c, pl.ds(base, 80), :]
            power = power + x * x
            placed_power = placed_power + p * p
        nine = []
        for part in (power, *beside_lanes(power, placed_power)):
            nine.extend(lines_three(part))
        mean_power = sum(nine[1:], nine[0]) / 9.0
        spread = jnp.zeros((64, 128), F32)
        for part in nine:
            spread = spread + (part - mean_power) ** 2
        spread = spread / 9.0
        gain = spread / (spread + 0.25 * mean_power * mean_power + 1.0)
        for c in range(6):
            x, p = xbuf[c, pl.ds(base, 80), :], pbuf[c, pl.ds(base, 80), :]
            left, right = beside_lanes(x, p)
            a, b, d = lines_three(left + x + right)
            local_mean = (a + b + d) / 9.0
            filtered = local_mean + gain * (x[8:72] - local_mean)
            fflat[pl.ds(tile * 8 + c, 64, stride=8), :] = filtered.astype(BF16).astype(F32)
        return 0

    lax.fori_loop(0, TILES // 64, filter_chunk, 0)

    for copy in w_copies:
        copy.wait()

    code_lane = iota((128, 256), 1)
    r = lax.rem(code_lane, 32)
    code = jnp.where(r < 3 * CAP, lax.div(lax.rem(code_lane, 128), 64) * 16 + lax.rem(r, CAP), -1)

    def block_copy(dst, peer_dst, sem):
        return pltpu.make_async_remote_copy(
            src_ref=payload.at[peer_dst], dst_ref=recv.at[dst], send_sem=send_sem, recv_sem=recv_sem.at[sem],
            device_id=(lax.div(peer_dst, N_SWATH), lax.rem(peer_dst, N_SWATH)), device_id_type=MESH,
        )

    def send_group(i, _):
        first = lax.rem(me + i * 13, DEVICES // 4) * 4
        for j in range(4):
            for k in range(CAP):
                v = fbuf[source[k, first + j]]
                vbuf[pl.ds(j * 64 + k, 3, stride=CAP), :] = v[0:3]
                vbuf[pl.ds(j * 64 + 32 + k, 3, stride=CAP), :] = v[3:6]
        v = vbuf[...].astype(BF16)
        zero = jnp.zeros((128, 128), BF16)
        rhs = jnp.concatenate(
            [jnp.concatenate([v[0:128], zero], axis=1), jnp.concatenate([zero, v[128:256]], axis=1)], axis=0
        )
        total = jnp.zeros((128, 256), F32)
        for jj in range(2):
            pairs = []
            for k in range(CAP):
                wa = wbuf[jnp.minimum(source[k, first + jj], TILES - 1)]
                wb = wbuf[jnp.minimum(source[k, first + 2 + jj], TILES - 1)]
                pairs.append(jnp.concatenate([wa, wb], axis=1))
            out = dot(jnp.concatenate(pairs, axis=0), rhs, NT)
            for k in range(CAP):
                total = jnp.where(code == jj * 16 + k, out[k * 128 : (k + 1) * 128], total)
        stage[0:128] = total[:, 0:128].T
        stage[128:256] = total[:, 128:256].T
        for j in range(4):
            o = first + j
            stage[j * 64 + MARK_ROW : j * 64 + MARK_ROW + 1, :] = marks[pl.ds(o, 1), :]
            payload[o] = stage[j * 64 : (j + 1) * 64, :].astype(BF16)
        for j in range(4):
            o = first + j

            @pl.when(o != me)
            def _():
                block_copy(me, o, me).start()

        return 0

    lax.fori_loop(0, DEVICES // 4, send_group, 0)
    own = pltpu.make_async_copy(payload.at[me], recv.at[me], recv_sem.at[me])
    own.start()

    lane = iota((1, 128), 1)
    line_row = iota((LS, 128), 0).astype(F32)

    def take_group(i, _):
        first = lax.rem(lax.div(me, 8) + i, DEVICES // 8) * 8
        for j in range(8):
            pltpu.make_async_copy(payload.at[0], recv.at[first + j], recv_sem.at[first + j]).wait()
        hot = []
        for q in range(2):
            line = jnp.zeros((1, 128), F32)
            for j in range(4):
                part = recv[first + q * 4 + j, 16:32, :].astype(F32)[MARK_ROW - 16 : MARK_ROW - 15]
                line = jnp.where(lax.div(lane, 32) == j, part, line)
            hot.append(jnp.where(line_row == line, 1.0, 0.0).astype(BF16))
        hot = jnp.concatenate(hot, axis=1)
        for h in range(2):
            block = recv[pl.ds(first, 8), h * 32 : (h + 1) * 32, :].reshape(256, 128)
            wide = jnp.concatenate([block * maskbuf[n] for n in range(6)], axis=1)
            map_ref[h] = map_ref[h] + dot(hot, wide)
        return 0

    lax.fori_loop(0, DEVICES // 8, take_group, 0)

    pr, pc = iota((128, 128), 0), iota((128, 128), 1)
    packed = jnp.zeros((LS, 128), F32)
    for n in range(12):
        z = map_ref[n // 6, :, (n % 6) * 128 : (n % 6 + 1) * 128]
        pick = jnp.where(((pr == 0) & (pc == n)) | ((pr == 127) & (pc == 16 + n)), 1.0, 0.0).astype(BF16)
        big = z.astype(BF16)
        rest = z - big.astype(F32)
        mid = rest.astype(BF16)
        small = (rest - mid.astype(F32)).astype(BF16)
        packed = packed + (dot(big, pick) + dot(mid, pick) + dot(small, pick))
        zrows[n : n + 1, :] = z[0:1]
        zrows[16 + n : 17 + n, :] = z[LS - 1 : LS]
    for n in range(12, 16):
        zrows[n : n + 1, :] = jnp.zeros((1, 128), F32)
        zrows[16 + n : 17 + n, :] = jnp.zeros((1, 128), F32)
    zedge[...] = packed.T[0:32]

    last = around(zedge, cols_ref, es_sem, er_sem)
    n = len(AROUND)
    for side_n, ds in enumerate((1, -1)):
        last.append(
            pltpu.make_async_remote_copy(
                src_ref=zrows, dst_ref=rows_ref.at[side_n], send_sem=es_sem.at[n], recv_sem=er_sem.at[n],
                device_id=beside(ds, 0), device_id_type=MESH,
            )
        )
        n += 1
    for copy in last:
        copy.start()
    for copy in last:
        copy.wait()
    pltpu.make_async_copy(payload.at[pl.ds(0, DEVICES - 1)], payload.at[pl.ds(0, DEVICES - 1)], send_sem).wait()


def fit_kernel(map_ref, cols_ref, rows_ref, fit_ref, out_ref, zplace, ztop, gbuf):
    sec, swath = lax.axis_index("sec"), lax.axis_index("swath")
    has_up, has_down = flag(sec > 0), flag(sec < N_SEC - 1)
    has_left, has_right = flag(swath > 0), flag(swath < N_SWATH - 1)
    low = iota((32, LS), 0) < 16
    side = jnp.where(low, has_right, has_left)

    def pick_sides(left_n, right_n):
        return jnp.where(low, cols_ref[right_n], cols_ref[left_n]) * side

    middle = pick_sides(0, 1)
    up, down = pick_sides(2, 3) * has_up, pick_sides(4, 5) * has_down
    corner_lane = iota((32, 128), 1)
    corners = jnp.where(corner_lane == 0, up[:, LS - 1 : LS], 0.0)
    corners = jnp.where(corner_lane == 1, down[:, 0:1], corners)
    lines_of = jnp.concatenate([middle, corners], axis=1)
    lines_of = jnp.concatenate([lines_of, jnp.zeros((96, LS + 128), F32)], axis=0).T
    big = lines_of.astype(BF16)
    rest = lines_of - big.astype(F32)
    mid = rest.astype(BF16)
    small = (rest - mid.astype(F32)).astype(BF16)
    pr, pc = iota((128, 128), 0), iota((128, 128), 1)
    for n in range(12):
        place = jnp.where(((pr == 16 + n) & (pc == 0)) | ((pr == n) & (pc == 127)), 1.0, 0.0).astype(BF16)
        placed = dot(big, place) + dot(mid, place) + dot(small, place)
        zplace[n, 0:LS] = placed[0:LS]
        zplace[n, LS : LS + 8] = placed[LS : LS + 8]
        ztop[n, 0:1] = rows_ref[0, 16 + n : 17 + n] * has_up
        ztop[n, 1:2] = rows_ref[1, n : n + 1] * has_down
        ztop[n, 2:8] = jnp.zeros((6, 128), F32)

    lane = iota((8, 128), 1)
    matrix = fit_ref[...]

    def block(z):
        parts = [z[i] * z[j] + z[6 + i] * z[6 + j] for i, j in upper_pairs]
        parts += [z[6 + i] * z[j] - z[i] * z[6 + j] for i, j in strict_pairs]
        joint = jnp.concatenate(parts, axis=0)
        high = joint.astype(BF16)
        rest_ = (joint - high.astype(F32)).astype(BF16)
        first = dot(matrix, high)
        g = first[0:128] + first[128:256] + dot(matrix[0:128], rest_)
        sums = []
        for k in range(16):
            g1, g2 = g[k * 8 : k * 8 + 8, 0:128], g[k * 8 : k * 8 + 8, 128:256]
            left = jnp.where(lane == 0, g2, pltpu.roll(g1, 1, 1))
            right = jnp.where(lane == 127, g2, pltpu.roll(g1, 127, 1))
            sums.append(left + g1 + right)
        return sums

    def step(b, _):
        at = pl.multiple_of(b * 8, 8)
        z = [
            jnp.concatenate(
                [
                    map_ref[n // 6, pl.ds(at, 8), (n % 6) * 128 : (n % 6 + 1) * 128],
                    zplace[n, pl.ds(at, 8), :],
                ],
                axis=1,
            )
            for n in range(12)
        ]
        for k, s in enumerate(block(z)):
            gbuf[k, pl.ds(at + 8, 8), :] = s
        return 0

    lax.fori_loop(0, LS // 8, step, 0)
    z = [jnp.concatenate([ztop[n], zplace[n, LS : LS + 8]], axis=1) for n in range(12)]
    for k, s in enumerate(block(z)):
        gbuf[k, 7:8, :] = s[0:1]
        gbuf[k, LS + 8 : LS + 9, :] = s[1:2]
    for k in range(16):
        out_ref[k] = gbuf[k, 7 : 7 + LS] + gbuf[k, 8 : 8 + LS] + gbuf[k, 9 : 9 + LS]


def vmem(n=1):
    return [pl.BlockSpec(memory_space=pltpu.VMEM)] * n


def body(radar_l, radar_s, weights_l, weights_s, owner_l, owner_s, slot_l, slot_s, models):
    source, marks, matrix = pl.pallas_call(
        plan_kernel,
        out_shape=(
            jax.ShapeDtypeStruct((16, DEVICES), I32),
            jax.ShapeDtypeStruct((DEVICES, 128), F32),
            jax.ShapeDtypeStruct((256, NJ * 8), BF16),
        ),
        in_specs=vmem(5),
        out_specs=vmem(3),
        compiler_params=pltpu.CompilerParams(vmem_limit_bytes=32 << 20),
        name="plan",
    )(owner_l, owner_s, slot_l.reshape(1, LL), slot_s.reshape(1, LS), models)
    dma, n_around = pltpu.SemaphoreType.DMA, len(AROUND)
    maps, cols, rows = pl.pallas_call(
        main_kernel,
        out_shape=(
            jax.ShapeDtypeStruct((2, LS, 768), F32),
            jax.ShapeDtypeStruct((n_around, 32, LS), F32),
            jax.ShapeDtypeStruct((2, 32, 128), F32),
        ),
        in_specs=vmem(2)
        + [pl.BlockSpec(memory_space=pl.ANY)] * 2
        + [pl.BlockSpec(memory_space=pltpu.SMEM)]
        + vmem(1),
        out_specs=vmem(3),
        scratch_shapes=[
            pltpu.VMEM((TILES, 128, 128), BF16),
            pltpu.VMEM((6, EXT, 128), F32),
            pltpu.VMEM((6, EXT, 128), F32),
            pltpu.VMEM((TILES + 1, 8, 128), F32),
            pltpu.VMEM((256, 128), F32),
            pltpu.VMEM((256, 128), F32),
            pltpu.VMEM((DEVICES, ROWS, 128), BF16),
            pltpu.VMEM((DEVICES, ROWS, 128), BF16),
            pltpu.VMEM((6, 256, 128), BF16),
            pltpu.VMEM((16, TILES), BF16),
            pltpu.VMEM((n_around, 16, TILES), BF16),
            pltpu.VMEM((2, 12, 16, 128), BF16),
            pltpu.VMEM((32, LS), F32),
            pltpu.VMEM((32, 128), F32),
            dma((8,)),
            dma((n_around + 4,)),
            dma((n_around + 4,)),
            dma,
            dma((DEVICES,)),
            dma((n_around + 2,)),
            dma((n_around + 2,)),
        ],
        compiler_params=pltpu.CompilerParams(
            collective_id=0, has_side_effects=True, vmem_limit_bytes=56 << 20
        ),
        name="unite",
    )(radar_l, radar_s, weights_l, weights_s, source, marks)
    return pl.pallas_call(
        fit_kernel,
        out_shape=jax.ShapeDtypeStruct((16, LS, 128), F32),
        in_specs=vmem(4),
        out_specs=vmem(1)[0],
        scratch_shapes=[
            pltpu.VMEM((12, LS + 8, 128), F32),
            pltpu.VMEM((12, 8, 128), F32),
            pltpu.VMEM((16, LS + 16, 128), F32),
        ],
        compiler_params=pltpu.CompilerParams(vmem_limit_bytes=32 << 20),
        name="fit",
    )(maps, cols, rows, matrix)


def solution(mesh):
    in_specs = (
        P(None, "sec", "swath"),
        P(None, "sec", "swath"),
        P(("sec", "swath"), None, None),
        P(("sec", "swath"), None, None),
        P(("sec", "swath"), None),
        P(("sec", "swath"), None),
        P(("sec", "swath")),
        P(("sec", "swath")),
        P(),
    )
    out_specs = P(None, "sec", "swath")
    return jax.shard_map(body, mesh=mesh, in_specs=in_specs, out_specs=out_specs, check_vma=False)
```

```python
import functools

import jax
import jax.numpy as jnp
from jax import lax
from jax.experimental import pallas as pl
from jax.experimental.pallas import tpu as pltpu
from jax.sharding import PartitionSpec as P

MESH = pl.DeviceIdType.MESH
F32, BF16, I32 = jnp.float32, jnp.bfloat16, jnp.int32
FIT_ITERS = 4
FIT_RATE = 0.25
N_SEC, N_SWATH, DEVICES = 4, 32, 128
LL, LS = 384, 256
CAP_L, CAP_S = 6, 4
CAP = CAP_L + CAP_S
TILES = LL + LS
ROWS = 64
MARK_ROW = 30
TOP_L, TOP_S = 8, 8 + LL + 16
EXT = LL + LS + 32
upper_pairs = [(i, j) for i in range(6) for j in range(i, 6)]
strict_pairs = [(i, j) for i in range(6) for j in range(i + 1, 6)]
NJ = len(upper_pairs) + len(strict_pairs)
AROUND = [(0, -1), (0, 1), (-1, -1), (-1, 1), (1, -1), (1, 1)]


def iota(shape, dim):
    return lax.broadcasted_iota(I32, shape, dim)


def dot(a, b, dims=((1,), (0,)), precision=None):
    return lax.dot_general(a, b, (dims, ((), ())), precision=precision, preferred_element_type=F32)


NT = ((1,), (1,))


def flag(cond):
    return jnp.where(cond, 1.0, 0.0).astype(F32)


def fill_plan(owner_l, owner_s, slot_l, slot_s, source_ref, marks_ref):
    rows, marks = [], []
    for owner, slot, lines, cap, first in ((owner_l, slot_l, LL, CAP_L, 0), (owner_s, slot_s, LS, CAP_S, LL)):
        hit = jnp.where(owner[...] == iota((DEVICES, lines), 0), 1.0, 0.0).astype(F32)
        earlier = jnp.where(iota((lines, lines), 0) < iota((lines, lines), 1), 1.0, 0.0).astype(BF16)
        before = dot(hit.astype(BF16), earlier)
        tile = iota((1, lines), 1) + first
        facts = jnp.concatenate(
            [
                slot[...].astype(F32),
                lax.rem(tile, 128).astype(F32),
                lax.div(tile, 128).astype(F32),
                jnp.ones((1, lines), F32),
                jnp.zeros((4, lines), F32),
            ],
            axis=0,
        ).astype(BF16)
        for k in range(cap):
            got = dot(facts, jnp.where(before == k, hit, 0.0).astype(BF16), NT)
            filled = got[3:4]
            rows.append(got[1:2] + 128.0 * got[2:3] + (1.0 - filled) * TILES)
            marks.append(got[0:1] + filled - 1.0)
    tiles = jnp.concatenate(rows + [jnp.zeros((16 - CAP, DEVICES), F32)], axis=0).astype(I32)
    source_ref[...] = jnp.clip(tiles, 0, TILES)
    table = jnp.concatenate(marks + [jnp.zeros((DEVICES - CAP, DEVICES), F32)], axis=0)
    lane = lax.rem(iota((DEVICES, 128), 1), 32)
    spread = jnp.where((lax.rem(lane, CAP) == iota((DEVICES, 128), 0)) & (lane < 3 * CAP), 1.0, 0.0).astype(BF16)
    marks_ref[...] = dot(table.T.astype(BF16), spread) - jnp.where(lane < 3 * CAP, 0.0, 1.0)


def fill_matrix(models, matrix_ref):
    high = lax.Precision.HIGHEST
    m = models[...]
    gram = dot(m, m, NT, precision=high)
    total = m
    for _ in range(FIT_ITERS - 1):
        total = m + total - FIT_RATE * dot(gram, total, precision=high)
    total = total * (FIT_RATE / 9.0)
    left = jnp.where(lax.div(iota((128, 16), 0), 8) == iota((128, 16), 1), 1.0, 0.0).astype(F32)
    right = jnp.where(lax.div(iota((NJ, NJ * 8), 1), 8) == iota((NJ, NJ * 8), 0), 1.0, 0.0).astype(F32)
    wide = dot(dot(left, total, precision=high), right, precision=high)
    same = lax.rem(iota((128, NJ * 8), 0), 8) == lax.rem(iota((128, NJ * 8), 1), 8)
    wide = jnp.where(same, wide, 0.0)
    big = wide.astype(BF16)
    matrix_ref[0:128] = big
    matrix_ref[128:256] = (wide - big.astype(F32)).astype(BF16)


def halves(x):
    big = x.astype(BF16)
    return jnp.concatenate([big, (x - big.astype(F32)).astype(BF16)], axis=1)


def joint_of(z):
    parts = [z[i] * z[j] + z[6 + i] * z[6 + j] for i, j in upper_pairs]
    parts += [z[6 + i] * z[j] - z[i] * z[6 + j] for i, j in strict_pairs]
    return jnp.concatenate(parts, axis=0)


def main_kernel(
    radar_l_hbm, radar_s_hbm, weights_l, weights_s, owner_l_hbm, owner_s_hbm, slot_l_hbm, slot_s_hbm, models_hbm,
    out_ref,
    radar_l, radar_s, owner_l, owner_s, slot_l, slot_s, models,
    wbuf, xbuf, pbuf, fbuf, vbuf, stage, payload, recv, maskbuf, edge, hcols, hrows,
    source_v, source, marks, matrix, zmap, zedge, zrows, zcols_in, zrows_in, zv, gbuf, gv, hbuf, halo_lines, obuf,
    in_sem, w_sem, hs_sem, hr_sem, send_sem, recv_sem, es_sem, er_sem, plan_sem, out_sem,
):
    sec, swath = lax.axis_index("sec"), lax.axis_index("swath")
    me = sec * N_SWATH + swath
    my_place = swath * N_SEC + sec

    pairs = (
        (radar_l_hbm, radar_l), (radar_s_hbm, radar_s), (owner_l_hbm, owner_l), (owner_s_hbm, owner_s),
        (slot_l_hbm, slot_l), (slot_s_hbm, slot_s), (models_hbm, models),
    )
    loads = [pltpu.make_async_copy(a, b, in_sem.at[n]) for n, (a, b) in enumerate(pairs)]
    for copy in loads:
        copy.start()

    barrier = pltpu.get_barrier_semaphore()

    def greet(i, _):
        peer = lax.rem(me + i, DEVICES)
        pl.semaphore_signal(
            barrier, inc=1, device_id=(lax.div(peer, N_SWATH), lax.rem(peer, N_SWATH)), device_id_type=MESH
        )
        return 0

    lax.fori_loop(1, DEVICES, greet, 0)
    for copy in loads:
        copy.wait()

    column, row = iota((16, 128), 1), iota((16, 128), 0)
    for radar, first, lines in ((radar_l, 0, LL), (radar_s, LL, LS)):
        total = jnp.zeros((16, lines), F32)
        for c in range(6):
            pick = jnp.where(
                ((row == c) & (column == 0)) | ((row == 8 + c) & (column == 127)), 1.0, 0.0
            ).astype(BF16)
            total = total + dot(pick, radar[c], NT)
        edge[:, first : first + lines] = total.astype(BF16)

    pl.semaphore_wait(barrier, DEVICES - 1)

    def beside(ds, dw):
        return (lax.rem(sec + ds + N_SEC, N_SEC), lax.rem(swath + dw + N_SWATH, N_SWATH))

    def around(src, slots, ssem, rsem):
        return [
            pltpu.make_async_remote_copy(
                src_ref=src, dst_ref=slots.at[n], send_sem=ssem.at[n], recv_sem=rsem.at[n],
                device_id=beside(-ds, -dw), device_id_type=MESH,
            )
            for n, (ds, dw) in enumerate(AROUND)
        ]

    halo = around(edge, hcols, hs_sem, hr_sem)
    n = len(AROUND)
    for radar, first, lines in ((radar_l, 0, LL), (radar_s, 6, LS)):
        for side, (start, ds) in enumerate(((lines - 16, 1), (0, -1))):
            halo.append(
                pltpu.make_async_remote_copy(
                    src_ref=radar.at[:, pl.ds(start, 16), :],
                    dst_ref=hrows.at[side, pl.ds(first, 6)],
                    send_sem=hs_sem.at[n], recv_sem=hr_sem.at[n],
                    device_id=beside(ds, 0), device_id_type=MESH,
                )
            )
            n += 1
    for copy in halo:
        copy.start()

    w_copies = []
    for n, (src, first, count) in enumerate(((weights_l, 0, LL), (weights_s, LL, LS))):
        for part in range(4):
            size = count // 4
            w_copies.append(
                pltpu.make_async_copy(
                    src.at[pl.ds(part * size, size)],
                    wbuf.at[pl.ds(first + part * size, size)],
                    w_sem.at[4 * n + part],
                )
            )
    for copy in w_copies:
        copy.start()

    fill_plan(owner_l, owner_s, slot_l, slot_s, source_v, marks)
    plan_copy = pltpu.make_async_copy(source_v, source, plan_sem)
    plan_copy.start()
    for radar, top, lines in ((radar_l, TOP_L, LL), (radar_s, TOP_S, LS)):
        for c in range(6):
            xbuf[c, top : top + lines, :] = radar[c].astype(F32)
    fbuf[TILES] = jnp.zeros((8, 128), F32)
    fflat = fbuf.reshape((TILES + 1) * 8, 128)
    vbuf[...] = jnp.zeros((256, 128), F32)
    zmap[...] = jnp.zeros((2, LS, 768), F32)
    r32 = lax.rem(iota((256, 128), 0), 32)
    for band in range(2):
        for c in range(3):
            k = r32 - 10 * c
            keep = (k >= 0) & (k < CAP_L) if band == 0 else (k >= CAP_L) & (k < CAP)
            maskbuf[band * 3 + c] = jnp.where(keep, 1.0, 0.0).astype(BF16)
    fill_matrix(models, matrix)

    for copy in halo:
        copy.wait()

    has_up, has_down = flag(sec > 0), flag(sec < N_SEC - 1)
    has_left, has_right = flag(swath > 0), flag(swath < N_SWATH - 1)
    low = iota((16, TILES), 0) < 8
    side = jnp.where(low, has_right, has_left)

    def pick_sides(left_n, right_n):
        return jnp.where(low, hcols[right_n].astype(F32), hcols[left_n].astype(F32)) * side

    middle = pick_sides(0, 1)
    up, down = pick_sides(2, 3) * has_up, pick_sides(4, 5) * has_down
    corner_lane = iota((16, 128), 1)
    corners = jnp.where(corner_lane == 0, up[:, LL - 1 : LL], 0.0)
    corners = jnp.where(corner_lane == 1, down[:, 0:1], corners)
    corners = jnp.where(corner_lane == 2, up[:, TILES - 1 : TILES], corners)
    corners = jnp.where(corner_lane == 3, down[:, LL : LL + 1], corners)
    lines_of = jnp.concatenate([middle, corners], axis=1)
    lines_of = jnp.concatenate([lines_of, jnp.zeros((112, TILES + 128), F32)], axis=0).T.astype(BF16)
    pr, pc = iota((128, 128), 0), iota((128, 128), 1)
    for c in range(6):
        place = jnp.where(((pr == 8 + c) & (pc == 0)) | ((pr == c) & (pc == 127)), 1.0, 0.0).astype(BF16)
        placed = dot(lines_of, place)
        pbuf[c, TOP_L : TOP_L + LL, :] = placed[0:LL]
        pbuf[c, TOP_S : TOP_S + LS, :] = placed[LL:TILES]
        pbuf[c, TOP_L - 1 : TOP_L, :] = placed[TILES : TILES + 1]
        pbuf[c, TOP_L + LL : TOP_L + LL + 1, :] = placed[TILES + 1 : TILES + 2]
        pbuf[c, TOP_S - 1 : TOP_S, :] = placed[TILES + 2 : TILES + 3]
        pbuf[c, TOP_S + LS : TOP_S + LS + 1, :] = placed[TILES + 3 : TILES + 4]
        for top, lines, first in ((TOP_L, LL, 0), (TOP_S, LS, 6)):
            xbuf[c, top - 1 : top, :] = hrows[0, first + c].astype(F32)[15:16] * has_up
            xbuf[c, top + lines : top + lines + 1, :] = hrows[1, first + c].astype(F32)[0:1] * has_down

    def beside_lanes(x, p):
        lane = iota(x.shape, 1)
        return (
            jnp.where(lane == 0, p, pltpu.roll(x, 1, 1)),
            jnp.where(lane == 127, p, pltpu.roll(x, 127, 1)),
        )

    def lines_three(h):
        return (pltpu.roll(h, 1, 0)[8:72], h[8:72], pltpu.roll(h, 79, 0)[8:72])

    def filter_chunk(i, _):
        base = pl.multiple_of(i * 64 + jnp.where(i >= LL // 64, 16, 0), 8)
        tile = i * 64
        power = jnp.zeros((80, 128), F32)
        placed_power = jnp.zeros((80, 128), F32)
        for c in range(6):
            x, p = xbuf[c, pl.ds(base, 80), :], pbuf[c, pl.ds(base, 80), :]
            power = power + x * x
            placed_power = placed_power + p * p
        nine = []
        for part in (power, *beside_lanes(power, placed_power)):
            nine.extend(lines_three(part))
        mean_power = sum(nine[1:], nine[0]) / 9.0
        spread = jnp.zeros((64, 128), F32)
        for part in nine:
            spread = spread + (part - mean_power) ** 2
        spread = spread / 9.0
        gain = spread / (spread + 0.25 * mean_power * mean_power + 1.0)
        for c in range(6):
            x, p = xbuf[c, pl.ds(base, 80), :], pbuf[c, pl.ds(base, 80), :]
            left, right = beside_lanes(x, p)
            a, b, d = lines_three(left + x + right)
            local_mean = (a + b + d) / 9.0
            filtered = local_mean + gain * (x[8:72] - local_mean)
            fflat[pl.ds(tile * 8 + c, 64, stride=8), :] = filtered.astype(BF16).astype(F32)
        return 0

    lax.fori_loop(0, TILES // 64, filter_chunk, 0)

    plan_copy.wait()
    for copy in w_copies:
        copy.wait()

    code_lane = iota((128, 256), 1)
    r = lax.rem(code_lane, 32)
    code = jnp.where(r < 3 * CAP, lax.div(lax.rem(code_lane, 128), 64) * 16 + lax.rem(r, CAP), -1)

    def send_group(i, _):
        first = lax.rem(swath + i * 13, DEVICES // 4) * 4
        for j in range(4):
            for k in range(CAP):
                v = fbuf[source[k, first + j]]
                vbuf[pl.ds(j * 64 + k, 3, stride=CAP), :] = v[0:3]
                vbuf[pl.ds(j * 64 + 32 + k, 3, stride=CAP), :] = v[3:6]
        v = vbuf[...].astype(BF16)
        zero = jnp.zeros((128, 128), BF16)
        rhs = jnp.concatenate(
            [jnp.concatenate([v[0:128], zero], axis=1), jnp.concatenate([zero, v[128:256]], axis=1)], axis=0
        )
        total = jnp.zeros((128, 256), F32)
        for jj in range(2):
            both = []
            for k in range(CAP):
                wa = wbuf[jnp.minimum(source[k, first + jj], TILES - 1)]
                wb = wbuf[jnp.minimum(source[k, first + 2 + jj], TILES - 1)]
                both.append(jnp.concatenate([wa, wb], axis=1))
            out = dot(jnp.concatenate(both, axis=0), rhs, NT)
            for k in range(CAP):
                total = jnp.where(code == jj * 16 + k, out[k * 128 : (k + 1) * 128], total)
        stage[0:128] = total[:, 0:128].T
        stage[128:256] = total[:, 128:256].T
        for j in range(4):
            o = first + j
            stage[j * 64 + MARK_ROW : j * 64 + MARK_ROW + 1, :] = marks[pl.ds(o, 1), :]
            payload[o] = stage[j * 64 : (j + 1) * 64, :].astype(BF16)
        for j in range(4):
            o = first + j

            @pl.when(o != me)
            def _():
                pltpu.make_async_remote_copy(
                    src_ref=payload.at[o], dst_ref=recv.at[my_place], send_sem=send_sem, recv_sem=recv_sem.at[my_place],
                    device_id=(lax.div(o, N_SWATH), lax.rem(o, N_SWATH)), device_id_type=MESH,
                ).start()

        return 0

    lax.fori_loop(0, DEVICES // 4, send_group, 0)
    own = pltpu.make_async_copy(payload.at[me], recv.at[my_place], recv_sem.at[my_place])
    own.start()

    mark_lane = iota((1, 128), 1)
    line_row = iota((LS, 128), 0).astype(F32)
    my_group = lax.div(me, 4)

    def take_group(i, _):
        starts = [
            pl.multiple_of(lax.rem(my_group + (2 * i + q) * 19, N_SWATH) * N_SEC, N_SEC) for q in range(2)
        ]
        hot = []
        for start in starts:
            for j in range(4):
                pltpu.make_async_copy(payload.at[0], recv.at[start + j], recv_sem.at[start + j]).wait()
        for start in starts:
            line = jnp.zeros((1, 128), F32)
            for j in range(4):
                part = recv[start + j, 16:32, :].astype(F32)[MARK_ROW - 16 : MARK_ROW - 15]
                line = jnp.where(lax.div(mark_lane, 32) == j, part, line)
            hot.append(jnp.where(line_row == line, 1.0, 0.0).astype(BF16))
        hot = jnp.concatenate(hot, axis=1)
        for h in range(2):
            block = jnp.concatenate(
                [recv[pl.ds(start, 4), h * 32 : (h + 1) * 32, :].reshape(128, 128) for start in starts], axis=0
            )
            wide = jnp.concatenate([block * maskbuf[n] for n in range(6)], axis=1)
            zmap[h] = zmap[h] + dot(hot, wide)
        return 0

    lax.fori_loop(0, DEVICES // 8, take_group, 0)

    packed = jnp.zeros((LS, 128), F32)
    qr, qc = lax.rem(iota((256, 128), 0), 128), iota((256, 128), 1)
    for n in range(12):
        z = zmap[n // 6, :, (n % 6) * 128 : (n % 6 + 1) * 128]
        pick = jnp.where(((qr == 0) & (qc == n)) | ((qr == 127) & (qc == 16 + n)), 1.0, 0.0).astype(BF16)
        packed = packed + dot(halves(z), pick)
        zrows[n : n + 1, :] = z[0:1]
        zrows[16 + n : 17 + n, :] = z[LS - 1 : LS]
    zrows[12:16, :] = jnp.zeros((4, 128), F32)
    zrows[28:32, :] = jnp.zeros((4, 128), F32)
    zedge[...] = packed.T[0:32]
    last = around(zedge, zcols_in, es_sem, er_sem)
    n = len(AROUND)
    for side_n, ds in enumerate((1, -1)):
        last.append(
            pltpu.make_async_remote_copy(
                src_ref=zrows, dst_ref=zrows_in.at[side_n], send_sem=es_sem.at[n], recv_sem=er_sem.at[n],
                device_id=beside(ds, 0), device_id_type=MESH,
            )
        )
        n += 1
    for copy in last:
        copy.start()

    def fit_lines(b, _):
        at = pl.multiple_of(b * 16, 16)
        both = []
        for part in range(2):
            z = [zmap[n // 6, pl.ds(at + part * 8, 8), (n % 6) * 128 : (n % 6 + 1) * 128] for n in range(12)]
            both.append(joint_of(z))
        g = dot(matrix[...], jnp.concatenate(both, axis=1).astype(BF16))
        g = g[0:128] + g[128:256]
        for k in range(16):
            gbuf[k, pl.ds(at, 8), :] = g[k * 8 : k * 8 + 8, 0:128]
            gbuf[k, pl.ds(at + 8, 8), :] = g[k * 8 : k * 8 + 8, 128:256]
        return 0

    lax.fori_loop(0, LS // 16, fit_lines, 0)

    for copy in last:
        copy.wait()

    low = iota((32, LS), 0) < 16
    side = jnp.where(low, has_right, has_left)

    def pick_map_sides(left_n, right_n):
        return jnp.where(low, zcols_in[right_n], zcols_in[left_n]) * side

    middle = pick_map_sides(0, 1)
    up, down = pick_map_sides(2, 3) * has_up, pick_map_sides(4, 5) * has_down
    corner_lane = iota((32, 128), 1)
    corners = jnp.where(lax.rem(corner_lane, 2) == 0, up[:, LS - 1 : LS], down[:, 0:1])
    for n in range(12):
        zv[n, 0:1] = middle[16 + n : 17 + n, 0:128]
        zv[n, 1:2] = middle[16 + n : 17 + n, 128:256]
        zv[n, 2:3] = middle[n : n + 1, 0:128]
        zv[n, 3:4] = middle[n : n + 1, 128:256]
        zv[n, 4:5] = jnp.where(mark_lane < 2, corners[16 + n : 17 + n], corners[n : n + 1])
        zv[n, 5:6] = zrows_in[0, 16 + n : 17 + n] * has_up
        zv[n, 6:7] = zrows_in[1, n : n + 1] * has_down
        zv[n, 7:8] = jnp.zeros((1, 128), F32)
    g = dot(matrix[...], joint_of([zv[n] for n in range(12)]).astype(BF16))
    g = g[0:128] + g[128:256]
    gv[...] = g
    corner = gv[pl.ds(4, 16, stride=8), :]
    lane16 = iota((16, 128), 1)
    for side_n in range(2):
        edge_line = gv[pl.ds(5 + side_n, 16, stride=8), :]
        left, right = corner[:, side_n : side_n + 1], corner[:, 2 + side_n : 3 + side_n]
        halo_lines[side_n] = (
            edge_line
            + jnp.where(lane16 == 0, left, pltpu.roll(edge_line, 1, 1))
            + jnp.where(lane16 == 127, right, pltpu.roll(edge_line, 127, 1))
        )
    turned = g.T
    turned = halves(jnp.concatenate([turned, pltpu.roll(turned, 127, 1)], axis=0))

    def finish(k, _):
        place = jnp.where(
            ((qr == k * 8) & (qc == 0)) | ((qr == k * 8 + 2) & (qc == 127)), 1.0, 0.0
        ).astype(BF16)
        beside_block = dot(turned, place)
        own_cells = gbuf[k]
        left, right = beside_lanes(own_cells, beside_block)
        hbuf[8 : 8 + LS] = own_cells + left + right
        hbuf[7:8] = halo_lines[0, pl.ds(k, 1), :]
        hbuf[8 + LS : 9 + LS] = halo_lines[1, pl.ds(k, 1), :]
        obuf[k] = hbuf[7 : 7 + LS] + hbuf[8 : 8 + LS] + hbuf[9 : 9 + LS]
        pltpu.make_async_copy(obuf.at[k], out_ref.at[k], out_sem.at[k]).start()
        return 0

    lax.fori_loop(0, 16, finish, 0)
    pltpu.make_async_copy(payload.at[pl.ds(0, DEVICES - 1)], payload.at[pl.ds(0, DEVICES - 1)], send_sem).wait()

    def written(k, _):
        pltpu.make_async_copy(obuf.at[k], out_ref.at[k], out_sem.at[k]).wait()
        return 0

    lax.fori_loop(0, 16, written, 0)


def body(radar_l, radar_s, weights_l, weights_s, owner_l, owner_s, slot_l, slot_s, models):
    dma, n_around = pltpu.SemaphoreType.DMA, len(AROUND)
    vmem = pltpu.VMEM
    return pl.pallas_call(
        main_kernel,
        out_shape=jax.ShapeDtypeStruct((16, LS, 128), F32),
        in_specs=[pl.BlockSpec(memory_space=pl.ANY)] * 9,
        out_specs=pl.BlockSpec(memory_space=pl.ANY),
        scratch_shapes=[
            vmem((6, LL, 128), BF16),
            vmem((6, LS, 128), BF16),
            vmem((1, LL), I32),
            vmem((1, LS), I32),
            vmem((1, LL), I32),
            vmem((1, LS), I32),
            vmem((16, NJ), F32),
            vmem((TILES, 128, 128), BF16),
            vmem((6, EXT, 128), F32),
            vmem((6, EXT, 128), F32),
            vmem((TILES + 1, 8, 128), F32),
            vmem((256, 128), F32),
            vmem((256, 128), F32),
            vmem((DEVICES, ROWS, 128), BF16),
            vmem((DEVICES, ROWS, 128), BF16),
            vmem((6, 256, 128), BF16),
            vmem((16, TILES), BF16),
            vmem((n_around, 16, TILES), BF16),
            vmem((2, 12, 16, 128), BF16),
            vmem((16, DEVICES), I32),
            pltpu.SMEM((16, DEVICES), I32),
            vmem((DEVICES, 128), F32),
            vmem((256, NJ * 8), BF16),
            vmem((2, LS, 768), F32),
            vmem((32, LS), F32),
            vmem((32, 128), F32),
            vmem((n_around, 32, LS), F32),
            vmem((2, 32, 128), F32),
            vmem((12, 8, 128), F32),
            vmem((16, LS, 128), F32),
            vmem((128, 128), F32),
            vmem((LS + 16, 128), F32),
            vmem((2, 16, 128), F32),
            vmem((16, LS, 128), F32),
            dma((7,)),
            dma((8,)),
            dma((n_around + 4,)),
            dma((n_around + 4,)),
            dma,
            dma((DEVICES,)),
            dma((n_around + 2,)),
            dma((n_around + 2,)),
            dma,
            dma((16,)),
        ],
        compiler_params=pltpu.CompilerParams(
            collective_id=0, has_side_effects=True, vmem_limit_bytes=60 << 20
        ),
        name="unite",
    )(
        radar_l, radar_s, weights_l, weights_s,
        owner_l.reshape(1, LL), owner_s.reshape(1, LS), slot_l.reshape(1, LL), slot_s.reshape(1, LS), models,
    )


def solution(mesh):
    in_specs = (
        P(None, "sec", "swath"),
        P(None, "sec", "swath"),
        P(("sec", "swath"), None, None),
        P(("sec", "swath"), None, None),
        P(("sec", "swath"), None),
        P(("sec", "swath"), None),
        P(("sec", "swath")),
        P(("sec", "swath")),
        P(),
    )
    out_specs = P(None, "sec", "swath")
    return jax.shard_map(body, mesh=mesh, in_specs=in_specs, out_specs=out_specs, check_vma=False)
```

```python
import functools

import jax
import jax.numpy as jnp
from jax import lax
from jax.experimental import pallas as pl
from jax.experimental.pallas import tpu as pltpu
from jax.sharding import PartitionSpec as P

MESH = pl.DeviceIdType.MESH
F32, BF16, I32 = jnp.float32, jnp.bfloat16, jnp.int32
FIT_ITERS = 4
FIT_RATE = 0.25
N_SEC, N_SWATH, DEVICES = 4, 32, 128
LL, LS = 384, 256
CAP_L, CAP_S = 6, 4
CAP = CAP_L + CAP_S
TILES = LL + LS
ROWS = 64
MARK_ROW = 30
FINISH = 4
TOP_L, TOP_S = 8, 8 + LL + 16
EXT = LL + LS + 32
upper_pairs = [(i, j) for i in range(6) for j in range(i, 6)]
strict_pairs = [(i, j) for i in range(6) for j in range(i + 1, 6)]
NJ = len(upper_pairs) + len(strict_pairs)
AROUND = [(0, -1), (0, 1), (-1, -1), (-1, 1), (1, -1), (1, 1)]


def iota(shape, dim):
    return lax.broadcasted_iota(I32, shape, dim)


def dot(a, b, dims=((1,), (0,)), precision=None):
    return lax.dot_general(a, b, (dims, ((), ())), precision=precision, preferred_element_type=F32)


NT = ((1,), (1,))


def flag(cond):
    return jnp.where(cond, 1.0, 0.0).astype(F32)


def fill_plan(owner_l, owner_s, slot_l, slot_s, source_ref, marks_ref):
    rows, marks = [], []
    for owner, slot, lines, cap, first in ((owner_l, slot_l, LL, CAP_L, 0), (owner_s, slot_s, LS, CAP_S, LL)):
        hit = jnp.where(owner[...] == iota((DEVICES, lines), 0), 1.0, 0.0).astype(F32)
        earlier = jnp.where(iota((lines, lines), 0) < iota((lines, lines), 1), 1.0, 0.0).astype(BF16)
        before = dot(hit.astype(BF16), earlier)
        tile = iota((1, lines), 1) + first
        facts = jnp.concatenate(
            [
                slot[...].reshape(1, lines).astype(F32),
                lax.rem(tile, 128).astype(F32),
                lax.div(tile, 128).astype(F32),
                jnp.ones((1, lines), F32),
                jnp.zeros((4, lines), F32),
            ],
            axis=0,
        ).astype(BF16)
        for k in range(cap):
            got = dot(facts, jnp.where(before == k, hit, 0.0).astype(BF16), NT)
            filled = got[3:4]
            rows.append(got[1:2] + 128.0 * got[2:3] + (1.0 - filled) * TILES)
            marks.append(got[0:1] + filled - 1.0)
    tiles = jnp.concatenate(rows + [jnp.zeros((16 - CAP, DEVICES), F32)], axis=0).astype(I32)
    source_ref[...] = jnp.clip(tiles, 0, TILES)
    table = jnp.concatenate(marks + [jnp.zeros((DEVICES - CAP, DEVICES), F32)], axis=0)
    lane = lax.rem(iota((DEVICES, 128), 1), 32)
    spread = jnp.where((lax.rem(lane, CAP) == iota((DEVICES, 128), 0)) & (lane < 3 * CAP), 1.0, 0.0).astype(BF16)
    marks_ref[...] = dot(table.T.astype(BF16), spread) - jnp.where(lane < 3 * CAP, 0.0, 1.0)


def fill_matrix(models, matrix_ref):
    high = lax.Precision.HIGHEST
    m = models[...]
    gram = dot(m, m, NT, precision=high)
    total = m
    for _ in range(FIT_ITERS - 1):
        total = m + total - FIT_RATE * dot(gram, total, precision=high)
    total = total * (FIT_RATE / 9.0)
    left = jnp.where(lax.div(iota((128, 16), 0), 8) == iota((128, 16), 1), 1.0, 0.0).astype(F32)
    right = jnp.where(lax.div(iota((NJ, NJ * 8), 1), 8) == iota((NJ, NJ * 8), 0), 1.0, 0.0).astype(F32)
    wide = dot(dot(left, total, precision=high), right, precision=high)
    same = lax.rem(iota((128, NJ * 8), 0), 8) == lax.rem(iota((128, NJ * 8), 1), 8)
    wide = jnp.where(same, wide, 0.0)
    big = wide.astype(BF16)
    matrix_ref[0:128] = big
    matrix_ref[128:256] = (wide - big.astype(F32)).astype(BF16)


def halves(x):
    big = x.astype(BF16)
    return jnp.concatenate([big, (x - big.astype(F32)).astype(BF16)], axis=1)


def beside_lanes(x, p):
    lane = iota(x.shape, 1)
    return (
        jnp.where(lane == 0, p, pltpu.roll(x, 1, 1)),
        jnp.where(lane == 127, p, pltpu.roll(x, 127, 1)),
    )


def joint_of(z):
    parts = [z[i] * z[j] + z[6 + i] * z[6 + j] for i, j in upper_pairs]
    parts += [z[6 + i] * z[j] - z[i] * z[6 + j] for i, j in strict_pairs]
    return jnp.concatenate(parts, axis=0)


def main_kernel(
    radar_l_hbm, radar_s_hbm, weights_l, weights_s, owner_l_hbm, owner_s_hbm, slot_l_hbm, slot_s_hbm, models_hbm,
    g_ref, turned_ref, halo_lines,
    radar_l, radar_s, owner_l, owner_s, slot_l, slot_s, models,
    wbuf, xbuf, pbuf, fbuf, stage, payload, recv, maskbuf, edge, hcols, hrows,
    source_v, source, marks, matrix, zmap, zedge, zrows, zcols_in, zrows_in, zv, gbuf, gv, hbuf,
    in_sem, w_sem, hs_sem, hr_sem, send_sem, recv_sem, es_sem, er_sem, plan_sem, out_sem,
):
    sec, swath = lax.axis_index("sec"), lax.axis_index("swath")
    me = sec * N_SWATH + swath
    turn = lax.rem(swath + sec * 8, N_SWATH)
    my_place = turn * N_SEC + sec

    pairs = (
        (radar_l_hbm, radar_l), (radar_s_hbm, radar_s), (owner_l_hbm, owner_l), (owner_s_hbm, owner_s),
        (slot_l_hbm, slot_l), (slot_s_hbm, slot_s), (models_hbm, models),
    )
    loads = [pltpu.make_async_copy(a, b, in_sem.at[n]) for n, (a, b) in enumerate(pairs)]
    for copy in loads:
        copy.start()

    barrier = pltpu.get_barrier_semaphore()

    def greet(ds, dw):
        peer = (lax.rem(sec + ds, N_SEC), lax.rem(swath + dw, N_SWATH))
        pl.semaphore_signal(barrier, inc=1, device_id=peer, device_id_type=MESH)

    for ds in range(1, N_SEC):
        greet(ds, 0)
    for dw in (1, N_SWATH - 1):
        for ds in range(N_SEC):
            greet(ds, dw)

    def greet_rest(dw, _):
        for ds in range(N_SEC):
            greet(ds, dw)
        return 0

    lax.fori_loop(2, N_SWATH - 1, greet_rest, 0)
    for copy in loads:
        copy.wait()

    column, row = iota((16, 128), 1), iota((16, 128), 0)
    for radar, first, lines in ((radar_l, 0, LL), (radar_s, LL, LS)):
        total = jnp.zeros((16, lines), F32)
        for c in range(6):
            pick = jnp.where(
                ((row == c) & (column == 0)) | ((row == 8 + c) & (column == 127)), 1.0, 0.0
            ).astype(BF16)
            total = total + dot(pick, radar[c], NT)
        edge[:, first : first + lines] = total.astype(BF16)

    pl.semaphore_wait(barrier, DEVICES - 1)

    def beside(ds, dw):
        return (lax.rem(sec + ds + N_SEC, N_SEC), lax.rem(swath + dw + N_SWATH, N_SWATH))

    def around(src, slots, ssem, rsem):
        return [
            pltpu.make_async_remote_copy(
                src_ref=src, dst_ref=slots.at[n], send_sem=ssem.at[n], recv_sem=rsem.at[n],
                device_id=beside(-ds, -dw), device_id_type=MESH,
            )
            for n, (ds, dw) in enumerate(AROUND)
        ]

    halo = around(edge, hcols, hs_sem, hr_sem)
    n = len(AROUND)
    for radar, first, lines in ((radar_l, 0, LL), (radar_s, 6, LS)):
        for side, (start, ds) in enumerate(((lines - 16, 1), (0, -1))):
            halo.append(
                pltpu.make_async_remote_copy(
                    src_ref=radar.at[:, pl.ds(start, 16), :],
                    dst_ref=hrows.at[side, pl.ds(first, 6)],
                    send_sem=hs_sem.at[n], recv_sem=hr_sem.at[n],
                    device_id=beside(ds, 0), device_id_type=MESH,
                )
            )
            n += 1
    for copy in halo:
        copy.start()

    w_copies = []
    for n, (src, first, count) in enumerate(((weights_l, 0, LL), (weights_s, LL, LS))):
        for part in range(4):
            size = count // 4
            w_copies.append(
                pltpu.make_async_copy(
                    src.at[pl.ds(part * size, size)],
                    wbuf.at[pl.ds(first + part * size, size)],
                    w_sem.at[4 * n + part],
                )
            )
    for copy in w_copies:
        copy.start()

    fill_plan(owner_l, owner_s, slot_l, slot_s, source_v, marks)
    plan_copy = pltpu.make_async_copy(source_v, source, plan_sem)
    plan_copy.start()
    for radar, top, lines in ((radar_l, TOP_L, LL), (radar_s, TOP_S, LS)):
        for c in range(6):
            xbuf[c, top : top + lines, :] = radar[c].astype(F32)
    fbuf[TILES] = jnp.zeros((8, 128), F32)
    fflat = fbuf.reshape((TILES + 1) * 8, 128)
    stage[...] = jnp.zeros((256, 128), F32)
    zmap[...] = jnp.zeros((2, LS, 768), F32)
    r32 = lax.rem(iota((256, 128), 0), 32)
    for band in range(2):
        for c in range(3):
            k = r32 - 10 * c
            keep = (k >= 0) & (k < CAP_L) if band == 0 else (k >= CAP_L) & (k < CAP)
            maskbuf[band * 3 + c] = jnp.where(keep, 1.0, 0.0).astype(BF16)
    fill_matrix(models, matrix)

    for copy in halo:
        copy.wait()

    has_up, has_down = flag(sec > 0), flag(sec < N_SEC - 1)
    has_left, has_right = flag(swath > 0), flag(swath < N_SWATH - 1)
    low = iota((16, TILES), 0) < 8
    side = jnp.where(low, has_right, has_left)

    def pick_sides(left_n, right_n):
        return jnp.where(low, hcols[right_n].astype(F32), hcols[left_n].astype(F32)) * side

    middle = pick_sides(0, 1)
    up, down = pick_sides(2, 3) * has_up, pick_sides(4, 5) * has_down
    corner_lane = iota((16, 128), 1)
    corners = jnp.where(corner_lane == 0, up[:, LL - 1 : LL], 0.0)
    corners = jnp.where(corner_lane == 1, down[:, 0:1], corners)
    corners = jnp.where(corner_lane == 2, up[:, TILES - 1 : TILES], corners)
    corners = jnp.where(corner_lane == 3, down[:, LL : LL + 1], corners)
    lines_of = jnp.concatenate([middle, corners], axis=1)
    lines_of = jnp.concatenate([lines_of, jnp.zeros((112, TILES + 128), F32)], axis=0).T.astype(BF16)
    pr, pc = iota((128, 128), 0), iota((128, 128), 1)
    for c in range(6):
        place = jnp.where(((pr == 8 + c) & (pc == 0)) | ((pr == c) & (pc == 127)), 1.0, 0.0).astype(BF16)
        placed = dot(lines_of, place)
        pbuf[c, TOP_L : TOP_L + LL, :] = placed[0:LL]
        pbuf[c, TOP_S : TOP_S + LS, :] = placed[LL:TILES]
        pbuf[c, TOP_L - 1 : TOP_L, :] = placed[TILES : TILES + 1]
        pbuf[c, TOP_L + LL : TOP_L + LL + 1, :] = placed[TILES + 1 : TILES + 2]
        pbuf[c, TOP_S - 1 : TOP_S, :] = placed[TILES + 2 : TILES + 3]
        pbuf[c, TOP_S + LS : TOP_S + LS + 1, :] = placed[TILES + 3 : TILES + 4]
        for top, lines, first in ((TOP_L, LL, 0), (TOP_S, LS, 6)):
            xbuf[c, top - 1 : top, :] = hrows[0, first + c].astype(F32)[15:16] * has_up
            xbuf[c, top + lines : top + lines + 1, :] = hrows[1, first + c].astype(F32)[0:1] * has_down

    def lines_three(h):
        return (pltpu.roll(h, 1, 0)[8:72], h[8:72], pltpu.roll(h, 79, 0)[8:72])

    def filter_chunk(i, _):
        base = pl.multiple_of(i * 64 + jnp.where(i >= LL // 64, 16, 0), 8)
        tile = i * 64
        power = jnp.zeros((80, 128), F32)
        placed_power = jnp.zeros((80, 128), F32)
        for c in range(6):
            x, p = xbuf[c, pl.ds(base, 80), :], pbuf[c, pl.ds(base, 80), :]
            power = power + x * x
            placed_power = placed_power + p * p
        nine = []
        for part in (power, *beside_lanes(power, placed_power)):
            nine.extend(lines_three(part))
        mean_power = sum(nine[1:], nine[0]) / 9.0
        spread = jnp.zeros((64, 128), F32)
        for part in nine:
            spread = spread + (part - mean_power) ** 2
        spread = spread / 9.0
        gain = spread / (spread + 0.25 * mean_power * mean_power + 1.0)
        for c in range(6):
            x, p = xbuf[c, pl.ds(base, 80), :], pbuf[c, pl.ds(base, 80), :]
            left, right = beside_lanes(x, p)
            a, b, d = lines_three(left + x + right)
            local_mean = (a + b + d) / 9.0
            filtered = local_mean + gain * (x[8:72] - local_mean)
            fflat[pl.ds(tile * 8 + c, 64, stride=8), :] = filtered.astype(BF16).astype(F32)
        for c in range(6, 8):
            fflat[pl.ds(tile * 8 + c, 64, stride=8), :] = jnp.zeros((64, 128), F32)
        return 0

    lax.fori_loop(0, TILES // 64, filter_chunk, 0)

    plan_copy.wait()
    for copy in w_copies:
        copy.wait()

    zero = jnp.zeros((16, 128), BF16)

    def send_group(i, _):
        first = lax.rem(turn + i * 13, DEVICES // 4) * 4
        for k in range(CAP):
            v = [fbuf[source[k, first + j]] for j in range(4)]
            w = [wbuf[jnp.minimum(source[k, first + j], TILES - 1)] for j in range(4)]
            top = jnp.concatenate([v[0], v[2]], axis=0).astype(BF16)
            bottom = jnp.concatenate([v[1], v[3]], axis=0).astype(BF16)
            lhs = jnp.concatenate(
                [jnp.concatenate([top, zero], axis=1), jnp.concatenate([zero, bottom], axis=1)], axis=0
            )
            rhs = jnp.concatenate(
                [jnp.concatenate([w[0], w[1]], axis=1), jnp.concatenate([w[2], w[3]], axis=1)], axis=0
            )
            out = dot(lhs, rhs, NT)
            for j, part in enumerate((out[0:8, 0:128], out[16:24, 0:128], out[8:16, 128:256], out[24:32, 128:256])):
                stage[pl.ds(j * 64 + k, 3, stride=CAP), :] = part[0:3]
                stage[pl.ds(j * 64 + 32 + k, 3, stride=CAP), :] = part[3:6]
        for j in range(4):
            o = first + j
            stage[j * 64 + MARK_ROW : j * 64 + MARK_ROW + 1, :] = marks[pl.ds(o, 1), :]
            payload[o] = stage[j * 64 : (j + 1) * 64, :].astype(BF16)
        for j in range(4):
            o = first + j

            @pl.when(o != me)
            def _():
                pltpu.make_async_remote_copy(
                    src_ref=payload.at[o], dst_ref=recv.at[my_place], send_sem=send_sem, recv_sem=recv_sem.at[my_place],
                    device_id=(lax.div(o, N_SWATH), lax.rem(o, N_SWATH)), device_id_type=MESH,
                ).start()

        return 0

    lax.fori_loop(0, DEVICES // 4, send_group, 0)
    own = pltpu.make_async_copy(payload.at[me], recv.at[my_place], recv_sem.at[my_place])
    own.start()

    mark_lane = iota((1, 128), 1)
    line_row = iota((LS, 128), 0).astype(F32)
    my_group = lax.div(me, 4)

    def take_group(i, _):
        starts = [
            pl.multiple_of(lax.rem(my_group + (2 * i + q) * 19, N_SWATH) * N_SEC, N_SEC) for q in range(2)
        ]
        hot = []
        for start in starts:
            for j in range(4):
                pltpu.make_async_copy(payload.at[0], recv.at[start + j], recv_sem.at[start + j]).wait()
        for start in starts:
            line = jnp.zeros((1, 128), F32)
            for j in range(4):
                part = recv[start + j, 16:32, :].astype(F32)[MARK_ROW - 16 : MARK_ROW - 15]
                line = jnp.where(lax.div(mark_lane, 32) == j, part, line)
            hot.append(jnp.where(line_row == line, 1.0, 0.0).astype(BF16))
        hot = jnp.concatenate(hot, axis=1)
        for h in range(2):
            block = jnp.concatenate(
                [recv[pl.ds(start, 4), h * 32 : (h + 1) * 32, :].reshape(128, 128) for start in starts], axis=0
            )
            wide = jnp.concatenate([block * maskbuf[n] for n in range(6)], axis=1)
            zmap[h] = zmap[h] + dot(hot, wide)
        return 0

    lax.fori_loop(0, DEVICES // 8, take_group, 0)

    packed = jnp.zeros((LS, 128), F32)
    qr, qc = lax.rem(iota((256, 128), 0), 128), iota((256, 128), 1)
    for n in range(12):
        z = zmap[n // 6, :, (n % 6) * 128 : (n % 6 + 1) * 128]
        pick = jnp.where(((qr == 0) & (qc == n)) | ((qr == 127) & (qc == 16 + n)), 1.0, 0.0).astype(BF16)
        packed = packed + dot(halves(z), pick)
        zrows[n : n + 1, :] = z[0:1]
        zrows[16 + n : 17 + n, :] = z[LS - 1 : LS]
    zrows[12:16, :] = jnp.zeros((4, 128), F32)
    zrows[28:32, :] = jnp.zeros((4, 128), F32)
    zedge[...] = packed.T[0:32]
    last = around(zedge, zcols_in, es_sem, er_sem)
    n = len(AROUND)
    for side_n, ds in enumerate((1, -1)):
        last.append(
            pltpu.make_async_remote_copy(
                src_ref=zrows, dst_ref=zrows_in.at[side_n], send_sem=es_sem.at[n], recv_sem=er_sem.at[n],
                device_id=beside(ds, 0), device_id_type=MESH,
            )
        )
        n += 1
    for copy in last:
        copy.start()

    def fit_lines(b, _):
        at = pl.multiple_of(b * 16, 16)
        both = []
        for part in range(2):
            z = [zmap[n // 6, pl.ds(at + part * 8, 8), (n % 6) * 128 : (n % 6 + 1) * 128] for n in range(12)]
            both.append(joint_of(z))
        g = dot(matrix[...], jnp.concatenate(both, axis=1).astype(BF16))
        g = g[0:128] + g[128:256]
        for k in range(16):
            gbuf[k, pl.ds(at, 8), :] = g[k * 8 : k * 8 + 8, 0:128]
            gbuf[k, pl.ds(at + 8, 8), :] = g[k * 8 : k * 8 + 8, 128:256]
        return 0

    lax.fori_loop(0, LS // 16, fit_lines, 0)
    hbuf[0:8] = jnp.zeros((8, 128), F32)
    hbuf[8 + LS : 16 + LS] = jnp.zeros((8, 128), F32)
    no_lane = jnp.zeros((LS, 128), F32)

    def window(k, _):
        cells = gbuf[k]
        left, right = beside_lanes(cells, no_lane)
        three = cells + left + right
        hbuf[8 : 8 + LS] = three
        gbuf[k] = hbuf[7 : 7 + LS] + three + hbuf[9 : 9 + LS]
        return 0

    lax.fori_loop(0, 16, window, 0)
    g_copy = pltpu.make_async_copy(gbuf, g_ref, out_sem)
    g_copy.start()

    for copy in last:
        copy.wait()

    low = iota((32, LS), 0) < 16
    side = jnp.where(low, has_right, has_left)

    def pick_map_sides(left_n, right_n):
        return jnp.where(low, zcols_in[right_n], zcols_in[left_n]) * side

    middle = pick_map_sides(0, 1)
    up, down = pick_map_sides(2, 3) * has_up, pick_map_sides(4, 5) * has_down
    corner_lane = iota((32, 128), 1)
    corners = jnp.where(lax.rem(corner_lane, 2) == 0, up[:, LS - 1 : LS], down[:, 0:1])
    for n in range(12):
        zv[n, 0:1] = middle[16 + n : 17 + n, 0:128]
        zv[n, 1:2] = middle[16 + n : 17 + n, 128:256]
        zv[n, 2:3] = middle[n : n + 1, 0:128]
        zv[n, 3:4] = middle[n : n + 1, 128:256]
        zv[n, 4:5] = jnp.where(mark_lane < 2, corners[16 + n : 17 + n], corners[n : n + 1])
        zv[n, 5:6] = zrows_in[0, 16 + n : 17 + n] * has_up
        zv[n, 6:7] = zrows_in[1, n : n + 1] * has_down
        zv[n, 7:8] = jnp.zeros((1, 128), F32)
    g = dot(matrix[...], joint_of([zv[n] for n in range(12)]).astype(BF16))
    g = g[0:128] + g[128:256]
    gv[...] = g
    corner = gv[pl.ds(4, 16, stride=8), :]
    lane16 = iota((16, 128), 1)
    for side_n in range(2):
        edge_line = gv[pl.ds(5 + side_n, 16, stride=8), :]
        left, right = corner[:, side_n : side_n + 1], corner[:, 2 + side_n : 3 + side_n]
        halo_lines[side_n] = (
            edge_line
            + jnp.where(lane16 == 0, left, pltpu.roll(edge_line, 1, 1))
            + jnp.where(lane16 == 127, right, pltpu.roll(edge_line, 127, 1))
        )
    turned = g.T
    columns = jnp.concatenate([turned, pltpu.roll(turned, 127, 1)], axis=0)
    hbuf[7:8] = jnp.zeros((1, 128), F32)
    hbuf[8 : 8 + LS] = columns
    hbuf[8 + LS : 9 + LS] = jnp.zeros((1, 128), F32)
    turned_ref[...] = halves(hbuf[7 : 7 + LS] + columns + hbuf[9 : 9 + LS])
    pltpu.make_async_copy(payload.at[pl.ds(0, DEVICES - 1)], payload.at[pl.ds(0, DEVICES - 1)], send_sem).wait()
    g_copy.wait()


def finish_kernel(cells_hbm, columns_hbm, lines_hbm, out_hbm, cells, columns, halo_lines, in_sem, small_sem, out_sem):
    small = [
        pltpu.make_async_copy(columns_hbm, columns, small_sem.at[0]),
        pltpu.make_async_copy(lines_hbm, halo_lines, small_sem.at[1]),
    ]
    parts = 16 // FINISH

    def moved(src, dst, sem):
        return [
            pltpu.make_async_copy(src.at[pl.ds(n * FINISH, FINISH)], dst.at[pl.ds(n * FINISH, FINISH)], sem.at[n])
            for n in range(parts)
        ]

    loads, stores = moved(cells_hbm, cells, in_sem), moved(cells, out_hbm, out_sem)
    for copy in small + loads:
        copy.start()
    for copy in small:
        copy.wait()
    qr, qc = lax.rem(iota((256, 128), 0), 128), iota((256, 128), 1)
    for n in range(parts):
        loads[n].wait()
        for k in range(n * FINISH, (n + 1) * FINISH):
            place = jnp.where(((qr == k * 8) & (qc == 0)) | ((qr == k * 8 + 2) & (qc == 127)), 1.0, 0.0).astype(BF16)
            cells[k] = cells[k] + dot(columns[...], place)
            cells[k, 0:1] = cells[k, 0:1] + halo_lines[0, k : k + 1]
            cells[k, LS - 1 : LS] = cells[k, LS - 1 : LS] + halo_lines[1, k : k + 1]
        stores[n].start()
    for copy in stores:
        copy.wait()


def body(radar_l, radar_s, weights_l, weights_s, owner_l, owner_s, slot_l, slot_s, models):
    dma, n_around = pltpu.SemaphoreType.DMA, len(AROUND)
    vmem = pltpu.VMEM
    cells, turned, halo_lines = pl.pallas_call(
        main_kernel,
        out_shape=(
            jax.ShapeDtypeStruct((16, LS, 128), F32),
            jax.ShapeDtypeStruct((256, 256), BF16),
            jax.ShapeDtypeStruct((2, 16, 128), F32),
        ),
        in_specs=[pl.BlockSpec(memory_space=pl.ANY)] * 9,
        out_specs=[pl.BlockSpec(memory_space=pl.ANY)] + [pl.BlockSpec(memory_space=pltpu.VMEM)] * 2,
        scratch_shapes=[
            vmem((6, LL, 128), BF16),
            vmem((6, LS, 128), BF16),
            vmem((1, LL), I32),
            vmem((1, LS), I32),
            vmem((LL,), I32),
            vmem((LS,), I32),
            vmem((16, NJ), F32),
            vmem((TILES, 128, 128), BF16),
            vmem((6, EXT, 128), F32),
            vmem((6, EXT, 128), F32),
            vmem((TILES + 1, 8, 128), F32),
            vmem((256, 128), F32),
            vmem((DEVICES, ROWS, 128), BF16),
            vmem((DEVICES, ROWS, 128), BF16),
            vmem((6, 256, 128), BF16),
            vmem((16, TILES), BF16),
            vmem((n_around, 16, TILES), BF16),
            vmem((2, 12, 16, 128), BF16),
            vmem((16, DEVICES), I32),
            pltpu.SMEM((16, DEVICES), I32),
            vmem((DEVICES, 128), F32),
            vmem((256, NJ * 8), BF16),
            vmem((2, LS, 768), F32),
            vmem((32, LS), F32),
            vmem((32, 128), F32),
            vmem((n_around, 32, LS), F32),
            vmem((2, 32, 128), F32),
            vmem((12, 8, 128), F32),
            vmem((16, LS, 128), F32),
            vmem((128, 128), F32),
            vmem((LS + 16, 128), F32),
            dma((7,)),
            dma((8,)),
            dma((n_around + 4,)),
            dma((n_around + 4,)),
            dma,
            dma((DEVICES,)),
            dma((n_around + 2,)),
            dma((n_around + 2,)),
            dma,
            dma,
        ],
        compiler_params=pltpu.CompilerParams(
            collective_id=0, has_side_effects=True, vmem_limit_bytes=60 << 20
        ),
        name="unite",
    )(
        radar_l, radar_s, weights_l, weights_s,
        owner_l.reshape(1, LL), owner_s.reshape(1, LS), slot_l, slot_s, models,
    )
    return pl.pallas_call(
        finish_kernel,
        out_shape=jax.ShapeDtypeStruct((16, LS, 128), F32),
        in_specs=[pl.BlockSpec(memory_space=pl.ANY)] * 3,
        out_specs=pl.BlockSpec(memory_space=pl.ANY),
        scratch_shapes=[
            vmem((16, LS, 128), F32),
            vmem((256, 256), BF16),
            vmem((2, 16, 128), F32),
            dma((16 // FINISH,)),
            dma((2,)),
            dma((16 // FINISH,)),
        ],
        compiler_params=pltpu.CompilerParams(vmem_limit_bytes=60 << 20),
        name="finish",
    )(cells, turned, halo_lines)


def solution(mesh):
    in_specs = (
        P(None, "sec", "swath"),
        P(None, "sec", "swath"),
        P(("sec", "swath"), None, None),
        P(("sec", "swath"), None, None),
        P(("sec", "swath"), None),
        P(("sec", "swath"), None),
        P(("sec", "swath")),
        P(("sec", "swath")),
        P(),
    )
    out_specs = P(None, "sec", "swath")
    return jax.shard_map(body, mesh=mesh, in_specs=in_specs, out_specs=out_specs, check_vma=False)
```

```python
import functools

import jax
import jax.numpy as jnp
from jax import lax
from jax.experimental import pallas as pl
from jax.experimental.pallas import tpu as pltpu
from jax.sharding import PartitionSpec as P

MESH = pl.DeviceIdType.MESH
F32, BF16, I32 = jnp.float32, jnp.bfloat16, jnp.int32
FIT_ITERS = 4
FIT_RATE = 0.25
N_SEC, N_SWATH, DEVICES = 4, 32, 128
LL, LS = 384, 256
CAP_L, CAP_S = 6, 4
CAP = CAP_L + CAP_S
TILES = LL + LS
ROWS = 64
MARK_ROW = 30
FINISH = 4
TOP_L, TOP_S = 8, 8 + LL + 16
EXT = LL + LS + 32
upper_pairs = [(i, j) for i in range(6) for j in range(i, 6)]
strict_pairs = [(i, j) for i in range(6) for j in range(i + 1, 6)]
NJ = len(upper_pairs) + len(strict_pairs)


def iota(shape, dim):
    return lax.broadcasted_iota(I32, shape, dim)


def dot(a, b, dims=((1,), (0,)), precision=None):
    return lax.dot_general(a, b, (dims, ((), ())), precision=precision, preferred_element_type=F32)


NT = ((1,), (1,))


def flag(cond):
    return jnp.where(cond, 1.0, 0.0).astype(F32)


def fill_plan(owner_l, owner_s, slot_l, slot_s, source_ref, marks_ref):
    rows, marks = [], []
    for owner, slot, lines, cap, first in ((owner_l, slot_l, LL, CAP_L, 0), (owner_s, slot_s, LS, CAP_S, LL)):
        hit = jnp.where(owner[...] == iota((DEVICES, lines), 0), 1.0, 0.0).astype(F32)
        earlier = jnp.where(iota((lines, lines), 0) < iota((lines, lines), 1), 1.0, 0.0).astype(BF16)
        before = dot(hit.astype(BF16), earlier)
        tile = iota((1, lines), 1) + first
        facts = jnp.concatenate(
            [
                slot[...].reshape(1, lines).astype(F32),
                lax.rem(tile, 128).astype(F32),
                lax.div(tile, 128).astype(F32),
                jnp.ones((1, lines), F32),
                jnp.zeros((4, lines), F32),
            ],
            axis=0,
        ).astype(BF16)
        for k in range(cap):
            got = dot(facts, jnp.where(before == k, hit, 0.0).astype(BF16), NT)
            filled = got[3:4]
            rows.append(got[1:2] + 128.0 * got[2:3] + (1.0 - filled) * TILES)
            marks.append(got[0:1] + filled - 1.0)
    tiles = jnp.concatenate(rows + [jnp.zeros((16 - CAP, DEVICES), F32)], axis=0).astype(I32)
    source_ref[...] = jnp.clip(tiles, 0, TILES)
    table = jnp.concatenate(marks + [jnp.zeros((DEVICES - CAP, DEVICES), F32)], axis=0)
    lane = lax.rem(iota((DEVICES, 128), 1), 32)
    spread = jnp.where((lax.rem(lane, CAP) == iota((DEVICES, 128), 0)) & (lane < 3 * CAP), 1.0, 0.0).astype(BF16)
    marks_ref[...] = dot(table.T.astype(BF16), spread) - jnp.where(lane < 3 * CAP, 0.0, 1.0)


def fill_matrix(models, matrix_ref):
    high = lax.Precision.HIGHEST
    m = models[...]
    gram = dot(m, m, NT, precision=high)
    total = m
    for _ in range(FIT_ITERS - 1):
        total = m + total - FIT_RATE * dot(gram, total, precision=high)
    total = total * (FIT_RATE / 9.0)
    left = jnp.where(lax.div(iota((128, 16), 0), 8) == iota((128, 16), 1), 1.0, 0.0).astype(F32)
    right = jnp.where(lax.div(iota((NJ, NJ * 8), 1), 8) == iota((NJ, NJ * 8), 0), 1.0, 0.0).astype(F32)
    wide = dot(dot(left, total, precision=high), right, precision=high)
    same = lax.rem(iota((128, NJ * 8), 0), 8) == lax.rem(iota((128, NJ * 8), 1), 8)
    wide = jnp.where(same, wide, 0.0)
    big = wide.astype(BF16)
    matrix_ref[0:128] = big
    matrix_ref[128:256] = (wide - big.astype(F32)).astype(BF16)


def halves(x):
    big = x.astype(BF16)
    return jnp.concatenate([big, (x - big.astype(F32)).astype(BF16)], axis=1)


def beside_lanes(x, p):
    lane = iota(x.shape, 1)
    return (
        jnp.where(lane == 0, p, pltpu.roll(x, 1, 1)),
        jnp.where(lane == 127, p, pltpu.roll(x, 127, 1)),
    )


def joint_of(z):
    parts = [z[i] * z[j] + z[6 + i] * z[6 + j] for i, j in upper_pairs]
    parts += [z[6 + i] * z[j] - z[i] * z[6 + j] for i, j in strict_pairs]
    return jnp.concatenate(parts, axis=0)


def main_kernel(
    radar_l_hbm, radar_s_hbm, weights_l, weights_s, owner_l_hbm, owner_s_hbm, slot_l_hbm, slot_s_hbm, models_hbm,
    g_ref, turned_ref, halo_lines,
    radar_l, radar_s, owner_l, owner_s, slot_l, slot_s, models,
    wbuf, xbuf, pbuf, fbuf, stage, payload, recv, maskbuf, edge, edge_rows, hcols, hcorners, hrows,
    source_v, source, marks, matrix, zmap, zedge, zrows, zcols_in, zcorners, zrows_in, zv, gbuf, gv, hbuf,
    in_sem, w_sem, hs_sem, hr_sem, send_sem, recv_sem, es_sem, er_sem, plan_sem, out_sem,
):
    sec, swath = lax.axis_index("sec"), lax.axis_index("swath")
    me = sec * N_SWATH + swath
    turn = lax.rem(swath + sec * 8, N_SWATH)
    my_place = turn * N_SEC + sec

    pairs = (
        (radar_l_hbm, radar_l), (radar_s_hbm, radar_s), (owner_l_hbm, owner_l), (owner_s_hbm, owner_s),
        (slot_l_hbm, slot_l), (slot_s_hbm, slot_s), (models_hbm, models),
    )
    loads = [pltpu.make_async_copy(a, b, in_sem.at[n]) for n, (a, b) in enumerate(pairs)]
    for copy in loads:
        copy.start()

    barrier = pltpu.get_barrier_semaphore()

    def greet(ds, dw):
        peer = (lax.rem(sec + ds, N_SEC), lax.rem(swath + dw, N_SWATH))
        pl.semaphore_signal(barrier, inc=1, device_id=peer, device_id_type=MESH)

    for ds in range(1, N_SEC):
        greet(ds, 0)
    for dw in (1, N_SWATH - 1):
        for ds in range(N_SEC):
            greet(ds, dw)

    def greet_rest(dw, _):
        for ds in range(N_SEC):
            greet(ds, dw)
        return 0

    lax.fori_loop(2, N_SWATH - 1, greet_rest, 0)
    for copy in loads:
        copy.wait()

    column, row = iota((16, 128), 1), iota((16, 128), 0)
    ends = jnp.zeros((16, 128), F32)
    for radar, first, lines in ((radar_l, 0, LL), (radar_s, LL, LS)):
        total = jnp.zeros((16, lines), F32)
        for c in range(6):
            pick = jnp.where(
                ((row == c) & (column == 0)) | ((row == 8 + c) & (column == 127)), 1.0, 0.0
            ).astype(BF16)
            total = total + dot(pick, radar[c], NT)
        edge[:, first : first + lines] = total.astype(BF16)
        at = 0 if first == 0 else 2
        ends = jnp.where(column == at, total[:, 0:1], ends)
        ends = jnp.where(column == at + 1, total[:, lines - 1 : lines], ends)
    edge[:, TILES : TILES + 128] = ends.astype(BF16)
    for end in range(2):
        lines_at_end = [
            radar[c, lines - 16 : lines, :].astype(F32)[15:16] if end else radar[c, 0:16, :].astype(F32)[0:1]
            for radar, lines in ((radar_l, LL), (radar_s, LS))
            for c in range(6)
        ]
        edge_rows[end] = jnp.concatenate(lines_at_end + [jnp.zeros((4, 128), F32)], axis=0).astype(BF16)

    pl.semaphore_wait(barrier, DEVICES - 1)

    def beside(ds, dw):
        return (lax.rem(sec + ds + N_SEC, N_SEC), lax.rem(swath + dw + N_SWATH, N_SWATH))

    def sends(moves, ssem, rsem):
        return [
            pltpu.make_async_remote_copy(
                src_ref=src, dst_ref=dst, send_sem=ssem.at[n], recv_sem=rsem.at[n],
                device_id=beside(ds, dw), device_id_type=MESH,
            )
            for n, (src, dst, ds, dw) in enumerate(moves)
        ]

    moves = [(edge.at[:, pl.ds(0, TILES)], hcols.at[0], 0, -1), (edge.at[:, pl.ds(0, TILES)], hcols.at[1], 0, 1)]
    for n, (ds, dw) in enumerate(((1, -1), (1, 1), (-1, -1), (-1, 1))):
        moves.append((edge.at[:, pl.ds(TILES, 128)], hcorners.at[n], ds, dw))
    moves += [(edge_rows.at[1], hrows.at[0], 1, 0), (edge_rows.at[0], hrows.at[1], -1, 0)]
    halo = sends(moves, hs_sem, hr_sem)
    for copy in halo:
        copy.start()

    w_copies = []
    for n, (src, first, count) in enumerate(((weights_l, 0, LL), (weights_s, LL, LS))):
        for part in range(4):
            size = count // 4
            w_copies.append(
                pltpu.make_async_copy(
                    src.at[pl.ds(part * size, size)],
                    wbuf.at[pl.ds(first + part * size, size)],
                    w_sem.at[4 * n + part],
                )
            )
    for copy in w_copies:
        copy.start()

    fill_plan(owner_l, owner_s, slot_l, slot_s, source_v, marks)
    plan_copy = pltpu.make_async_copy(source_v, source, plan_sem)
    plan_copy.start()
    for radar, top, lines in ((radar_l, TOP_L, LL), (radar_s, TOP_S, LS)):
        for c in range(6):
            xbuf[c, top : top + lines, :] = radar[c].astype(F32)
    fbuf[TILES] = jnp.zeros((8, 128), F32)
    fflat = fbuf.reshape((TILES + 1) * 8, 128)
    stage[...] = jnp.zeros((256, 128), F32)
    zmap[...] = jnp.zeros((2, LS, 768), F32)
    r32 = lax.rem(iota((256, 128), 0), 32)
    for band in range(2):
        for c in range(3):
            k = r32 - 10 * c
            keep = (k >= 0) & (k < CAP_L) if band == 0 else (k >= CAP_L) & (k < CAP)
            maskbuf[band * 3 + c] = jnp.where(keep, 1.0, 0.0).astype(BF16)
    fill_matrix(models, matrix)

    for copy in halo:
        copy.wait()

    has_up, has_down = flag(sec > 0), flag(sec < N_SEC - 1)
    has_left, has_right = flag(swath > 0), flag(swath < N_SWATH - 1)

    def merge(right, left):
        low = iota(right.shape, 0) < 8
        return jnp.where(low, right.astype(F32) * has_right, left.astype(F32) * has_left)

    middle = merge(hcols[0], hcols[1])
    up = merge(hcorners[0], hcorners[1]) * has_up
    down = merge(hcorners[2], hcorners[3]) * has_down
    corners = jnp.where(column == 0, up[:, 1:2], 0.0)
    corners = jnp.where(column == 1, down[:, 0:1], corners)
    corners = jnp.where(column == 2, up[:, 3:4], corners)
    corners = jnp.where(column == 3, down[:, 2:3], corners)
    lines_of = jnp.concatenate([middle, corners], axis=1)
    lines_of = jnp.concatenate([lines_of, jnp.zeros((112, TILES + 128), F32)], axis=0).T.astype(BF16)
    pr, pc = iota((128, 128), 0), iota((128, 128), 1)
    above, below = hrows[0].astype(F32) * has_up, hrows[1].astype(F32) * has_down
    for c in range(6):
        place = jnp.where(((pr == 8 + c) & (pc == 0)) | ((pr == c) & (pc == 127)), 1.0, 0.0).astype(BF16)
        placed = dot(lines_of, place)
        pbuf[c, TOP_L : TOP_L + LL, :] = placed[0:LL]
        pbuf[c, TOP_S : TOP_S + LS, :] = placed[LL:TILES]
        pbuf[c, TOP_L - 1 : TOP_L, :] = placed[TILES : TILES + 1]
        pbuf[c, TOP_L + LL : TOP_L + LL + 1, :] = placed[TILES + 1 : TILES + 2]
        pbuf[c, TOP_S - 1 : TOP_S, :] = placed[TILES + 2 : TILES + 3]
        pbuf[c, TOP_S + LS : TOP_S + LS + 1, :] = placed[TILES + 3 : TILES + 4]
        for top, lines, first in ((TOP_L, LL, 0), (TOP_S, LS, 6)):
            xbuf[c, top - 1 : top, :] = above[first + c : first + c + 1]
            xbuf[c, top + lines : top + lines + 1, :] = below[first + c : first + c + 1]

    def lines_three(h):
        return (pltpu.roll(h, 1, 0)[8:72], h[8:72], pltpu.roll(h, 79, 0)[8:72])

    def filter_chunk(i, _):
        base = pl.multiple_of(i * 64 + jnp.where(i >= LL // 64, 16, 0), 8)
        tile = i * 64
        power = jnp.zeros((80, 128), F32)
        placed_power = jnp.zeros((80, 128), F32)
        for c in range(6):
            x, p = xbuf[c, pl.ds(base, 80), :], pbuf[c, pl.ds(base, 80), :]
            power = power + x * x
            placed_power = placed_power + p * p
        nine = []
        for part in (power, *beside_lanes(power, placed_power)):
            nine.extend(lines_three(part))
        mean_power = sum(nine[1:], nine[0]) / 9.0
        spread = jnp.zeros((64, 128), F32)
        for part in nine:
            spread = spread + (part - mean_power) ** 2
        spread = spread / 9.0
        gain = spread / (spread + 0.25 * mean_power * mean_power + 1.0)
        for c in range(6):
            x, p = xbuf[c, pl.ds(base, 80), :], pbuf[c, pl.ds(base, 80), :]
            left, right = beside_lanes(x, p)
            a, b, d = lines_three(left + x + right)
            local_mean = (a + b + d) / 9.0
            filtered = local_mean + gain * (x[8:72] - local_mean)
            fflat[pl.ds(tile * 8 + c, 64, stride=8), :] = filtered.astype(BF16).astype(F32)
        for c in range(6, 8):
            fflat[pl.ds(tile * 8 + c, 64, stride=8), :] = jnp.zeros((64, 128), F32)
        return 0

    lax.fori_loop(0, TILES // 64, filter_chunk, 0)

    plan_copy.wait()
    for copy in w_copies:
        copy.wait()

    zero = jnp.zeros((16, 128), BF16)

    def send_group(i, _):
        first = lax.rem(turn + i * 13, DEVICES // 4) * 4
        for k in range(CAP):
            v = [fbuf[source[k, first + j]] for j in range(4)]
            w = [wbuf[jnp.minimum(source[k, first + j], TILES - 1)] for j in range(4)]
            top = jnp.concatenate([v[0], v[2]], axis=0).astype(BF16)
            bottom = jnp.concatenate([v[1], v[3]], axis=0).astype(BF16)
            lhs = jnp.concatenate(
                [jnp.concatenate([top, zero], axis=1), jnp.concatenate([zero, bottom], axis=1)], axis=0
            )
            rhs = jnp.concatenate(
                [jnp.concatenate([w[0], w[1]], axis=1), jnp.concatenate([w[2], w[3]], axis=1)], axis=0
            )
            out = dot(lhs, rhs, NT)
            for j, part in enumerate((out[0:8, 0:128], out[16:24, 0:128], out[8:16, 128:256], out[24:32, 128:256])):
                stage[pl.ds(j * 64 + k, 3, stride=CAP), :] = part[0:3]
                stage[pl.ds(j * 64 + 32 + k, 3, stride=CAP), :] = part[3:6]
        for j in range(4):
            o = first + j
            stage[j * 64 + MARK_ROW : j * 64 + MARK_ROW + 1, :] = marks[pl.ds(o, 1), :]
            payload[o] = stage[j * 64 : (j + 1) * 64, :].astype(BF16)
        for j in range(4):
            o = first + j

            @pl.when(o != me)
            def _():
                pltpu.make_async_remote_copy(
                    src_ref=payload.at[o], dst_ref=recv.at[my_place], send_sem=send_sem, recv_sem=recv_sem.at[my_place],
                    device_id=(lax.div(o, N_SWATH), lax.rem(o, N_SWATH)), device_id_type=MESH,
                ).start()

        return 0

    lax.fori_loop(0, DEVICES // 4, send_group, 0)
    own = pltpu.make_async_copy(payload.at[me], recv.at[my_place], recv_sem.at[my_place])
    own.start()

    mark_lane = iota((1, 128), 1)
    line_row = iota((LS, 128), 0).astype(F32)
    my_group = lax.div(me, 4)

    def take_group(i, _):
        starts = [
            pl.multiple_of(lax.rem(my_group + (2 * i + q) * 19, N_SWATH) * N_SEC, N_SEC) for q in range(2)
        ]
        hot = []
        for start in starts:
            for j in range(4):
                pltpu.make_async_copy(payload.at[0], recv.at[start + j], recv_sem.at[start + j]).wait()
        for start in starts:
            line = jnp.zeros((1, 128), F32)
            for j in range(4):
                part = recv[start + j, 16:32, :].astype(F32)[MARK_ROW - 16 : MARK_ROW - 15]
                line = jnp.where(lax.div(mark_lane, 32) == j, part, line)
            hot.append(jnp.where(line_row == line, 1.0, 0.0).astype(BF16))
        hot = jnp.concatenate(hot, axis=1)
        for h in range(2):
            block = jnp.concatenate(
                [recv[pl.ds(start, 4), h * 32 : (h + 1) * 32, :].reshape(128, 128) for start in starts], axis=0
            )
            wide = jnp.concatenate([block * maskbuf[n] for n in range(6)], axis=1)
            zmap[h] = zmap[h] + dot(hot, wide)
        return 0

    lax.fori_loop(0, DEVICES // 8, take_group, 0)

    packed = jnp.zeros((LS, 128), F32)
    qr, qc = lax.rem(iota((256, 128), 0), 128), iota((256, 128), 1)
    for n in range(12):
        z = zmap[n // 6, :, (n % 6) * 128 : (n % 6 + 1) * 128]
        pick = jnp.where(((qr == 0) & (qc == n)) | ((qr == 127) & (qc == 16 + n)), 1.0, 0.0).astype(BF16)
        packed = packed + dot(halves(z), pick)
        zrows[n : n + 1, :] = z[0:1]
        zrows[16 + n : 17 + n, :] = z[LS - 1 : LS]
    zrows[12:16, :] = jnp.zeros((4, 128), F32)
    zrows[28:32, :] = jnp.zeros((4, 128), F32)
    turned_edges = packed.T[0:32]
    zedge[:, 0:LS] = turned_edges
    corner_lane = iota((32, 128), 1)
    zedge[:, LS : LS + 128] = jnp.where(corner_lane == 0, turned_edges[:, 0:1], turned_edges[:, LS - 1 : LS])
    moves = [
        (zedge.at[pl.ds(0, 16), pl.ds(0, LS)], zcols_in.at[pl.ds(0, 16)], 0, -1),
        (zedge.at[pl.ds(16, 16), pl.ds(0, LS)], zcols_in.at[pl.ds(16, 16)], 0, 1),
    ]
    for n, (ds, dw) in enumerate(((1, -1), (1, 1), (-1, -1), (-1, 1))):
        part = pl.ds((n % 2) * 16, 16)
        moves.append((zedge.at[part, pl.ds(LS, 128)], zcorners.at[n // 2, part], ds, dw))
    moves += [
        (zrows.at[pl.ds(16, 16)], zrows_in.at[0], 1, 0),
        (zrows.at[pl.ds(0, 16)], zrows_in.at[1], -1, 0),
    ]
    last = sends(moves, es_sem, er_sem)
    for copy in last:
        copy.start()

    def fit_lines(b, _):
        at = pl.multiple_of(b * 16, 16)
        both = []
        for part in range(2):
            z = [zmap[n // 6, pl.ds(at + part * 8, 8), (n % 6) * 128 : (n % 6 + 1) * 128] for n in range(12)]
            both.append(joint_of(z))
        g = dot(matrix[...], jnp.concatenate(both, axis=1).astype(BF16))
        g = g[0:128] + g[128:256]
        for k in range(16):
            gbuf[k, pl.ds(at, 8), :] = g[k * 8 : k * 8 + 8, 0:128]
            gbuf[k, pl.ds(at + 8, 8), :] = g[k * 8 : k * 8 + 8, 128:256]
        return 0

    lax.fori_loop(0, LS // 16, fit_lines, 0)
    hbuf[0:8] = jnp.zeros((8, 128), F32)
    hbuf[8 + LS : 16 + LS] = jnp.zeros((8, 128), F32)
    no_lane = jnp.zeros((LS, 128), F32)

    def window(k, _):
        cells = gbuf[k]
        left, right = beside_lanes(cells, no_lane)
        three = cells + left + right
        hbuf[8 : 8 + LS] = three
        gbuf[k] = hbuf[7 : 7 + LS] + three + hbuf[9 : 9 + LS]
        return 0

    g_copies = []
    for n in range(4):
        lax.fori_loop(n * 4, n * 4 + 4, window, 0)
        g_copies.append(
            pltpu.make_async_copy(gbuf.at[pl.ds(n * 4, 4)], g_ref.at[pl.ds(n * 4, 4)], out_sem.at[n])
        )
        g_copies[-1].start()

    for copy in last:
        copy.wait()

    side = jnp.where(iota((32, 1), 0) < 16, has_right, has_left)
    middle = zcols_in[...] * side
    up, down = zcorners[0] * (side * has_up), zcorners[1] * (side * has_down)
    corners = jnp.where(lax.rem(corner_lane, 2) == 0, up[:, 1:2], down[:, 0:1])
    for n in range(12):
        zv[n, 0:1] = middle[16 + n : 17 + n, 0:128]
        zv[n, 1:2] = middle[16 + n : 17 + n, 128:256]
        zv[n, 2:3] = middle[n : n + 1, 0:128]
        zv[n, 3:4] = middle[n : n + 1, 128:256]
        zv[n, 4:5] = jnp.where(mark_lane < 2, corners[16 + n : 17 + n], corners[n : n + 1])
        zv[n, 5:6] = zrows_in[0, n : n + 1] * has_up
        zv[n, 6:7] = zrows_in[1, n : n + 1] * has_down
        zv[n, 7:8] = jnp.zeros((1, 128), F32)
    g = dot(matrix[...], joint_of([zv[n] for n in range(12)]).astype(BF16))
    g = g[0:128] + g[128:256]
    gv[...] = g
    corner = gv[pl.ds(4, 16, stride=8), :]
    lane16 = iota((16, 128), 1)
    for side_n in range(2):
        edge_line = gv[pl.ds(5 + side_n, 16, stride=8), :]
        left, right = corner[:, side_n : side_n + 1], corner[:, 2 + side_n : 3 + side_n]
        halo_lines[side_n] = (
            edge_line
            + jnp.where(lane16 == 0, left, pltpu.roll(edge_line, 1, 1))
            + jnp.where(lane16 == 127, right, pltpu.roll(edge_line, 127, 1))
        )
    turned = g.T
    columns = jnp.concatenate([turned, pltpu.roll(turned, 127, 1)], axis=0)
    hbuf[7:8] = jnp.zeros((1, 128), F32)
    hbuf[8 : 8 + LS] = columns
    hbuf[8 + LS : 9 + LS] = jnp.zeros((1, 128), F32)
    turned_ref[...] = halves(hbuf[7 : 7 + LS] + columns + hbuf[9 : 9 + LS])
    pltpu.make_async_copy(payload.at[pl.ds(0, DEVICES - 1)], payload.at[pl.ds(0, DEVICES - 1)], send_sem).wait()
    for copy in g_copies:
        copy.wait()


def finish_kernel(cells_hbm, columns_hbm, lines_hbm, out_hbm, cells, columns, halo_lines, in_sem, small_sem, out_sem):
    small = [
        pltpu.make_async_copy(columns_hbm, columns, small_sem.at[0]),
        pltpu.make_async_copy(lines_hbm, halo_lines, small_sem.at[1]),
    ]
    parts = 16 // FINISH

    def moved(src, dst, sem):
        return [
            pltpu.make_async_copy(src.at[pl.ds(n * FINISH, FINISH)], dst.at[pl.ds(n * FINISH, FINISH)], sem.at[n])
            for n in range(parts)
        ]

    loads, stores = moved(cells_hbm, cells, in_sem), moved(cells, out_hbm, out_sem)
    for copy in small + loads:
        copy.start()
    for copy in small:
        copy.wait()
    qr, qc = lax.rem(iota((256, 128), 0), 128), iota((256, 128), 1)
    for n in range(parts):
        loads[n].wait()
        for k in range(n * FINISH, (n + 1) * FINISH):
            place = jnp.where(((qr == k * 8) & (qc == 0)) | ((qr == k * 8 + 2) & (qc == 127)), 1.0, 0.0).astype(BF16)
            cells[k] = cells[k] + dot(columns[...], place)
            cells[k, 0:1] = cells[k, 0:1] + halo_lines[0, k : k + 1]
            cells[k, LS - 1 : LS] = cells[k, LS - 1 : LS] + halo_lines[1, k : k + 1]
        stores[n].start()
    for copy in stores:
        copy.wait()


def body(radar_l, radar_s, weights_l, weights_s, owner_l, owner_s, slot_l, slot_s, models):
    dma = pltpu.SemaphoreType.DMA
    vmem = pltpu.VMEM
    cells, turned, halo_lines = pl.pallas_call(
        main_kernel,
        out_shape=(
            jax.ShapeDtypeStruct((16, LS, 128), F32),
            jax.ShapeDtypeStruct((256, 256), BF16),
            jax.ShapeDtypeStruct((2, 16, 128), F32),
        ),
        in_specs=[pl.BlockSpec(memory_space=pl.ANY)] * 9,
        out_specs=[pl.BlockSpec(memory_space=pl.ANY)] + [pl.BlockSpec(memory_space=pltpu.VMEM)] * 2,
        scratch_shapes=[
            vmem((6, LL, 128), BF16),
            vmem((6, LS, 128), BF16),
            vmem((1, LL), I32),
            vmem((1, LS), I32),
            vmem((LL,), I32),
            vmem((LS,), I32),
            vmem((16, NJ), F32),
            vmem((TILES, 128, 128), BF16),
            vmem((6, EXT, 128), F32),
            vmem((6, EXT, 128), F32),
            vmem((TILES + 1, 8, 128), F32),
            vmem((256, 128), F32),
            vmem((DEVICES, ROWS, 128), BF16),
            vmem((DEVICES, ROWS, 128), BF16),
            vmem((6, 256, 128), BF16),
            vmem((16, TILES + 128), BF16),
            vmem((2, 16, 128), BF16),
            vmem((2, 16, TILES), BF16),
            vmem((4, 16, 128), BF16),
            vmem((2, 16, 128), BF16),
            vmem((16, DEVICES), I32),
            pltpu.SMEM((16, DEVICES), I32),
            vmem((DEVICES, 128), F32),
            vmem((256, NJ * 8), BF16),
            vmem((2, LS, 768), F32),
            vmem((32, LS + 128), F32),
            vmem((32, 128), F32),
            vmem((32, LS), F32),
            vmem((2, 32, 128), F32),
            vmem((2, 16, 128), F32),
            vmem((12, 8, 128), F32),
            vmem((16, LS, 128), F32),
            vmem((128, 128), F32),
            vmem((LS + 16, 128), F32),
            dma((7,)),
            dma((8,)),
            dma((8,)),
            dma((8,)),
            dma,
            dma((DEVICES,)),
            dma((8,)),
            dma((8,)),
            dma,
            dma((4,)),
        ],
        compiler_params=pltpu.CompilerParams(
            collective_id=0, has_side_effects=True, vmem_limit_bytes=60 << 20
        ),
        name="unite",
    )(
        radar_l, radar_s, weights_l, weights_s,
        owner_l.reshape(1, LL), owner_s.reshape(1, LS), slot_l, slot_s, models,
    )
    return pl.pallas_call(
        finish_kernel,
        out_shape=jax.ShapeDtypeStruct((16, LS, 128), F32),
        in_specs=[pl.BlockSpec(memory_space=pl.ANY)] * 3,
        out_specs=pl.BlockSpec(memory_space=pl.ANY),
        scratch_shapes=[
            vmem((16, LS, 128), F32),
            vmem((256, 256), BF16),
            vmem((2, 16, 128), F32),
            dma((16 // FINISH,)),
            dma((2,)),
            dma((16 // FINISH,)),
        ],
        compiler_params=pltpu.CompilerParams(vmem_limit_bytes=60 << 20),
        name="finish",
    )(cells, turned, halo_lines)


def solution(mesh):
    in_specs = (
        P(None, "sec", "swath"),
        P(None, "sec", "swath"),
        P(("sec", "swath"), None, None),
        P(("sec", "swath"), None, None),
        P(("sec", "swath"), None),
        P(("sec", "swath"), None),
        P(("sec", "swath")),
        P(("sec", "swath")),
        P(),
    )
    out_specs = P(None, "sec", "swath")
    return jax.shard_map(body, mesh=mesh, in_specs=in_specs, out_specs=out_specs, check_vma=False)
```

```python
import functools

import jax
import jax.numpy as jnp
from jax import lax
from jax.experimental import pallas as pl
from jax.experimental.pallas import tpu as pltpu
from jax.sharding import PartitionSpec as P

MESH = pl.DeviceIdType.MESH
F32, BF16, I32 = jnp.float32, jnp.bfloat16, jnp.int32
FIT_ITERS = 4
FIT_RATE = 0.25
N_SEC, N_SWATH, DEVICES = 4, 32, 128
LL, LS = 384, 256
CAP_L, CAP_S = 6, 4
CAP = CAP_L + CAP_S
TILES = LL + LS
ROWS = 64
MARK_ROW = 30
FINISH = 4
TOP_L, TOP_S = 8, 8 + LL + 16
EXT = LL + LS + 32
upper_pairs = [(i, j) for i in range(6) for j in range(i, 6)]
strict_pairs = [(i, j) for i in range(6) for j in range(i + 1, 6)]
NJ = len(upper_pairs) + len(strict_pairs)


def iota(shape, dim):
    return lax.broadcasted_iota(I32, shape, dim)


def dot(a, b, dims=((1,), (0,)), precision=None):
    return lax.dot_general(a, b, (dims, ((), ())), precision=precision, preferred_element_type=F32)


NT = ((1,), (1,))


def flag(cond):
    return jnp.where(cond, 1.0, 0.0).astype(F32)


def fill_plan(owner_l, owner_s, slot_l, slot_s, source_ref, marks_ref):
    rows, marks = [], []
    for owner, slot, lines, cap, first in ((owner_l, slot_l, LL, CAP_L, 0), (owner_s, slot_s, LS, CAP_S, LL)):
        hit = jnp.where(owner[...] == iota((DEVICES, lines), 0), 1.0, 0.0).astype(F32)
        earlier = jnp.where(iota((lines, lines), 0) < iota((lines, lines), 1), 1.0, 0.0).astype(BF16)
        before = dot(hit.astype(BF16), earlier)
        tile = iota((1, lines), 1) + first
        facts = jnp.concatenate(
            [
                slot[...].reshape(1, lines).astype(F32),
                lax.rem(tile, 128).astype(F32),
                lax.div(tile, 128).astype(F32),
                jnp.ones((1, lines), F32),
                jnp.zeros((4, lines), F32),
            ],
            axis=0,
        ).astype(BF16)
        for k in range(cap):
            got = dot(facts, jnp.where(before == k, hit, 0.0).astype(BF16), NT)
            filled = got[3:4]
            rows.append(got[1:2] + 128.0 * got[2:3] + (1.0 - filled) * TILES)
            marks.append(got[0:1] + filled - 1.0)
    tiles = jnp.concatenate(rows + [jnp.zeros((16 - CAP, DEVICES), F32)], axis=0).astype(I32)
    source_ref[...] = jnp.clip(tiles, 0, TILES)
    table = jnp.concatenate(marks + [jnp.zeros((DEVICES - CAP, DEVICES), F32)], axis=0)
    lane = lax.rem(iota((DEVICES, 128), 1), 32)
    spread = jnp.where((lax.rem(lane, CAP) == iota((DEVICES, 128), 0)) & (lane < 3 * CAP), 1.0, 0.0).astype(BF16)
    marks_ref[...] = dot(table.T.astype(BF16), spread) - jnp.where(lane < 3 * CAP, 0.0, 1.0)


def fill_matrix(models, matrix_ref):
    high = lax.Precision.HIGHEST
    m = models[...]
    gram = dot(m, m, NT, precision=high)
    total = m
    for _ in range(FIT_ITERS - 1):
        total = m + total - FIT_RATE * dot(gram, total, precision=high)
    total = total * (FIT_RATE / 9.0)
    left = jnp.where(lax.div(iota((128, 16), 0), 8) == iota((128, 16), 1), 1.0, 0.0).astype(F32)
    right = jnp.where(lax.div(iota((NJ, NJ * 8), 1), 8) == iota((NJ, NJ * 8), 0), 1.0, 0.0).astype(F32)
    wide = dot(dot(left, total, precision=high), right, precision=high)
    same = lax.rem(iota((128, NJ * 8), 0), 8) == lax.rem(iota((128, NJ * 8), 1), 8)
    wide = jnp.where(same, wide, 0.0)
    big = wide.astype(BF16)
    matrix_ref[0:128] = big
    matrix_ref[128:256] = (wide - big.astype(F32)).astype(BF16)


def halves(x):
    big = x.astype(BF16)
    return jnp.concatenate([big, (x - big.astype(F32)).astype(BF16)], axis=1)


def beside_lanes(x, p):
    lane = iota(x.shape, 1)
    return (
        jnp.where(lane == 0, p, pltpu.roll(x, 1, 1)),
        jnp.where(lane == 127, p, pltpu.roll(x, 127, 1)),
    )


def joint_of(z):
    parts = [z[i] * z[j] + z[6 + i] * z[6 + j] for i, j in upper_pairs]
    parts += [z[6 + i] * z[j] - z[i] * z[6 + j] for i, j in strict_pairs]
    return jnp.concatenate(parts, axis=0)


def main_kernel(
    radar_l_hbm, radar_s_hbm, weights_l, weights_s, owner_l_hbm, owner_s_hbm, slot_l_hbm, slot_s_hbm, models_hbm,
    g_ref, turned_ref, halo_lines,
    radar_l, radar_s, owner_l, owner_s, slot_l, slot_s, models,
    wbuf, xbuf, pbuf, fbuf, stage, payload, recv, maskbuf, edge, edge_rows, hcols, hcorners, hrows,
    source_v, source, marks, matrix, zmap, zedge, zrows, zcols_in, zcorners, zrows_in, zv, gbuf, gv, hbuf,
    in_sem, w_sem, hs_sem, hr_sem, send_sem, recv_sem, es_sem, er_sem, plan_sem, out_sem,
):
    sec, swath = lax.axis_index("sec"), lax.axis_index("swath")
    me = sec * N_SWATH + swath
    turn = lax.rem(swath + sec * 8, N_SWATH)
    my_place = turn * N_SEC + sec

    pairs = (
        (radar_l_hbm, radar_l), (radar_s_hbm, radar_s), (owner_l_hbm, owner_l), (owner_s_hbm, owner_s),
        (slot_l_hbm, slot_l), (slot_s_hbm, slot_s), (models_hbm, models),
    )
    loads = [pltpu.make_async_copy(a, b, in_sem.at[n]) for n, (a, b) in enumerate(pairs)]
    for copy in loads:
        copy.start()

    barrier = pltpu.get_barrier_semaphore()

    def greet(ds, dw):
        peer = (lax.rem(sec + ds, N_SEC), lax.rem(swath + dw, N_SWATH))
        pl.semaphore_signal(barrier, inc=1, device_id=peer, device_id_type=MESH)

    for ds in range(1, N_SEC):
        greet(ds, 0)
    for dw in (1, N_SWATH - 1):
        for ds in range(N_SEC):
            greet(ds, dw)

    def greet_rest(dw, _):
        for ds in range(N_SEC):
            greet(ds, dw)
        return 0

    lax.fori_loop(2, N_SWATH - 1, greet_rest, 0)
    for copy in loads:
        copy.wait()

    column, row = iota((16, 128), 1), iota((16, 128), 0)
    ends = jnp.zeros((16, 128), F32)
    for radar, first, lines in ((radar_l, 0, LL), (radar_s, LL, LS)):
        total = jnp.zeros((16, lines), F32)
        for c in range(6):
            pick = jnp.where(
                ((row == c) & (column == 0)) | ((row == 8 + c) & (column == 127)), 1.0, 0.0
            ).astype(BF16)
            total = total + dot(pick, radar[c], NT)
        edge[:, first : first + lines] = total.astype(BF16)
        at = 0 if first == 0 else 2
        ends = jnp.where(column == at, total[:, 0:1], ends)
        ends = jnp.where(column == at + 1, total[:, lines - 1 : lines], ends)
    edge[:, TILES : TILES + 128] = ends.astype(BF16)
    for end in range(2):
        lines_at_end = [
            radar[c, lines - 16 : lines, :].astype(F32)[15:16] if end else radar[c, 0:16, :].astype(F32)[0:1]
            for radar, lines in ((radar_l, LL), (radar_s, LS))
            for c in range(6)
        ]
        edge_rows[end] = jnp.concatenate(lines_at_end + [jnp.zeros((4, 128), F32)], axis=0).astype(BF16)

    pl.semaphore_wait(barrier, DEVICES - 1)

    def beside(ds, dw):
        return (lax.rem(sec + ds + N_SEC, N_SEC), lax.rem(swath + dw + N_SWATH, N_SWATH))

    def sends(moves, ssem, rsem):
        return [
            pltpu.make_async_remote_copy(
                src_ref=src, dst_ref=dst, send_sem=ssem.at[n], recv_sem=rsem.at[n],
                device_id=beside(ds, dw), device_id_type=MESH,
            )
            for n, (src, dst, ds, dw) in enumerate(moves)
        ]

    moves = [(edge.at[:, pl.ds(0, TILES)], hcols.at[0], 0, -1), (edge.at[:, pl.ds(0, TILES)], hcols.at[1], 0, 1)]
    for n, (ds, dw) in enumerate(((1, -1), (1, 1), (-1, -1), (-1, 1))):
        moves.append((edge.at[:, pl.ds(TILES, 128)], hcorners.at[n], ds, dw))
    moves += [(edge_rows.at[1], hrows.at[0], 1, 0), (edge_rows.at[0], hrows.at[1], -1, 0)]
    halo = sends(moves, hs_sem, hr_sem)
    for copy in halo:
        copy.start()

    w_copies = []
    for n, (src, first, count) in enumerate(((weights_l, 0, LL), (weights_s, LL, LS))):
        for part in range(4):
            size = count // 4
            w_copies.append(
                pltpu.make_async_copy(
                    src.at[pl.ds(part * size, size)],
                    wbuf.at[pl.ds(first + part * size, size)],
                    w_sem.at[4 * n + part],
                )
            )
    for copy in w_copies:
        copy.start()

    fill_plan(owner_l, owner_s, slot_l, slot_s, source_v, marks)
    plan_copy = pltpu.make_async_copy(source_v, source, plan_sem)
    plan_copy.start()
    for radar, top, lines in ((radar_l, TOP_L, LL), (radar_s, TOP_S, LS)):
        for c in range(6):
            xbuf[c, top : top + lines, :] = radar[c].astype(F32)
    fbuf[TILES] = jnp.zeros((8, 128), F32)
    fflat = fbuf.reshape((TILES + 1) * 8, 128)
    stage[...] = jnp.zeros((256, 128), F32)
    zmap[...] = jnp.zeros((2, LS, 768), F32)
    r32 = lax.rem(iota((256, 128), 0), 32)
    for band in range(2):
        for c in range(3):
            k = r32 - 10 * c
            keep = (k >= 0) & (k < CAP_L) if band == 0 else (k >= CAP_L) & (k < CAP)
            maskbuf[band * 3 + c] = jnp.where(keep, 1.0, 0.0).astype(BF16)
    fill_matrix(models, matrix)

    for copy in halo:
        copy.wait()

    has_up, has_down = flag(sec > 0), flag(sec < N_SEC - 1)
    has_left, has_right = flag(swath > 0), flag(swath < N_SWATH - 1)

    def merge(right, left):
        low = iota(right.shape, 0) < 8
        return jnp.where(low, right.astype(F32) * has_right, left.astype(F32) * has_left)

    middle = merge(hcols[0], hcols[1])
    up = merge(hcorners[0], hcorners[1]) * has_up
    down = merge(hcorners[2], hcorners[3]) * has_down
    corners = jnp.where(column == 0, up[:, 1:2], 0.0)
    corners = jnp.where(column == 1, down[:, 0:1], corners)
    corners = jnp.where(column == 2, up[:, 3:4], corners)
    corners = jnp.where(column == 3, down[:, 2:3], corners)
    lines_of = jnp.concatenate([middle, corners], axis=1)
    lines_of = jnp.concatenate([lines_of, jnp.zeros((112, TILES + 128), F32)], axis=0).T.astype(BF16)
    pr, pc = iota((128, 128), 0), iota((128, 128), 1)
    above, below = hrows[0].astype(F32) * has_up, hrows[1].astype(F32) * has_down
    for c in range(6):
        place = jnp.where(((pr == 8 + c) & (pc == 0)) | ((pr == c) & (pc == 127)), 1.0, 0.0).astype(BF16)
        placed = dot(lines_of, place)
        pbuf[c, TOP_L : TOP_L + LL, :] = placed[0:LL]
        pbuf[c, TOP_S : TOP_S + LS, :] = placed[LL:TILES]
        pbuf[c, TOP_L - 1 : TOP_L, :] = placed[TILES : TILES + 1]
        pbuf[c, TOP_L + LL : TOP_L + LL + 1, :] = placed[TILES + 1 : TILES + 2]
        pbuf[c, TOP_S - 1 : TOP_S, :] = placed[TILES + 2 : TILES + 3]
        pbuf[c, TOP_S + LS : TOP_S + LS + 1, :] = placed[TILES + 3 : TILES + 4]
        for top, lines, first in ((TOP_L, LL, 0), (TOP_S, LS, 6)):
            xbuf[c, top - 1 : top, :] = above[first + c : first + c + 1]
            xbuf[c, top + lines : top + lines + 1, :] = below[first + c : first + c + 1]

    def lines_three(h):
        return (pltpu.roll(h, 1, 0)[8:72], h[8:72], pltpu.roll(h, 79, 0)[8:72])

    def filter_chunk(i, _):
        base = pl.multiple_of(i * 64 + jnp.where(i >= LL // 64, 16, 0), 8)
        tile = i * 64
        power = jnp.zeros((80, 128), F32)
        placed_power = jnp.zeros((80, 128), F32)
        for c in range(6):
            x, p = xbuf[c, pl.ds(base, 80), :], pbuf[c, pl.ds(base, 80), :]
            power = power + x * x
            placed_power = placed_power + p * p
        nine = []
        for part in (power, *beside_lanes(power, placed_power)):
            nine.extend(lines_three(part))
        mean_power = sum(nine[1:], nine[0]) / 9.0
        spread = jnp.zeros((64, 128), F32)
        for part in nine:
            spread = spread + (part - mean_power) ** 2
        spread = spread / 9.0
        gain = spread / (spread + 0.25 * mean_power * mean_power + 1.0)
        for c in range(6):
            x, p = xbuf[c, pl.ds(base, 80), :], pbuf[c, pl.ds(base, 80), :]
            left, right = beside_lanes(x, p)
            a, b, d = lines_three(left + x + right)
            local_mean = (a + b + d) / 9.0
            filtered = local_mean + gain * (x[8:72] - local_mean)
            fflat[pl.ds(tile * 8 + c, 64, stride=8), :] = filtered.astype(BF16).astype(F32)
        for c in range(6, 8):
            fflat[pl.ds(tile * 8 + c, 64, stride=8), :] = jnp.zeros((64, 128), F32)
        return 0

    lax.fori_loop(0, TILES // 64, filter_chunk, 0)

    plan_copy.wait()
    for copy in w_copies:
        copy.wait()

    zero = jnp.zeros((16, 128), BF16)

    def send_group(i, _):
        first = lax.rem(turn + i * 13, DEVICES // 4) * 4
        for k in range(CAP):
            v = [fbuf[source[k, first + j]] for j in range(4)]
            w = [wbuf[jnp.minimum(source[k, first + j], TILES - 1)] for j in range(4)]
            top = jnp.concatenate([v[0], v[2]], axis=0).astype(BF16)
            bottom = jnp.concatenate([v[1], v[3]], axis=0).astype(BF16)
            lhs = jnp.concatenate(
                [jnp.concatenate([top, zero], axis=1), jnp.concatenate([zero, bottom], axis=1)], axis=0
            )
            rhs = jnp.concatenate(
                [jnp.concatenate([w[0], w[1]], axis=1), jnp.concatenate([w[2], w[3]], axis=1)], axis=0
            )
            out = dot(lhs, rhs, NT)
            for j, part in enumerate((out[0:8, 0:128], out[16:24, 0:128], out[8:16, 128:256], out[24:32, 128:256])):
                stage[pl.ds(j * 64 + k, 3, stride=CAP), :] = part[0:3]
                stage[pl.ds(j * 64 + 32 + k, 3, stride=CAP), :] = part[3:6]
        for j in range(4):
            o = first + j
            stage[j * 64 + MARK_ROW : j * 64 + MARK_ROW + 1, :] = marks[pl.ds(o, 1), :]
            payload[o] = stage[j * 64 : (j + 1) * 64, :].astype(BF16)
        for j in range(4):
            o = first + j

            @pl.when(o != me)
            def _():
                pltpu.make_async_remote_copy(
                    src_ref=payload.at[o], dst_ref=recv.at[my_place], send_sem=send_sem, recv_sem=recv_sem.at[my_place],
                    device_id=(lax.div(o, N_SWATH), lax.rem(o, N_SWATH)), device_id_type=MESH,
                ).start()

        return 0

    lax.fori_loop(0, DEVICES // 4, send_group, 0)
    own = pltpu.make_async_copy(payload.at[me], recv.at[my_place], recv_sem.at[my_place])
    own.start()

    mark_lane = iota((1, 128), 1)
    line_row = iota((LS, 128), 0).astype(F32)
    my_group = lax.div(me, 4)

    def take_group(i, _):
        starts = [
            pl.multiple_of(lax.rem(my_group + (2 * i + q) * 19, N_SWATH) * N_SEC, N_SEC) for q in range(2)
        ]
        hot = []
        for start in starts:
            for j in range(4):
                pltpu.make_async_copy(payload.at[0], recv.at[start + j], recv_sem.at[start + j]).wait()
        for start in starts:
            line = jnp.zeros((1, 128), F32)
            for j in range(4):
                part = recv[start + j, 16:32, :].astype(F32)[MARK_ROW - 16 : MARK_ROW - 15]
                line = jnp.where(lax.div(mark_lane, 32) == j, part, line)
            hot.append(jnp.where(line_row == line, 1.0, 0.0).astype(BF16))
        hot = jnp.concatenate(hot, axis=1)
        for h in range(2):
            block = jnp.concatenate(
                [recv[pl.ds(start, 4), h * 32 : (h + 1) * 32, :].reshape(128, 128) for start in starts], axis=0
            )
            wide = jnp.concatenate([block * maskbuf[n] for n in range(6)], axis=1)
            zmap[h] = zmap[h] + dot(hot, wide)
        return 0

    lax.fori_loop(0, DEVICES // 8, take_group, 0)

    packed = jnp.zeros((LS, 128), F32)
    qr, qc = lax.rem(iota((256, 128), 0), 128), iota((256, 128), 1)
    for n in range(12):
        z = zmap[n // 6, :, (n % 6) * 128 : (n % 6 + 1) * 128]
        pick = jnp.where(((qr == 0) & (qc == n)) | ((qr == 127) & (qc == 16 + n)), 1.0, 0.0).astype(BF16)
        packed = packed + dot(halves(z), pick)
        zrows[n : n + 1, :] = z[0:1]
        zrows[16 + n : 17 + n, :] = z[LS - 1 : LS]
    zrows[12:16, :] = jnp.zeros((4, 128), F32)
    zrows[28:32, :] = jnp.zeros((4, 128), F32)
    turned_edges = packed.T[0:32]
    zedge[:, 0:LS] = turned_edges
    corner_lane = iota((32, 128), 1)
    zedge[:, LS : LS + 128] = jnp.where(corner_lane == 0, turned_edges[:, 0:1], turned_edges[:, LS - 1 : LS])
    moves = [
        (zedge.at[pl.ds(0, 16), pl.ds(0, LS)], zcols_in.at[pl.ds(0, 16)], 0, -1),
        (zedge.at[pl.ds(16, 16), pl.ds(0, LS)], zcols_in.at[pl.ds(16, 16)], 0, 1),
    ]
    for n, (ds, dw) in enumerate(((1, -1), (1, 1), (-1, -1), (-1, 1))):
        part = pl.ds((n % 2) * 16, 16)
        moves.append((zedge.at[part, pl.ds(LS, 128)], zcorners.at[n // 2, part], ds, dw))
    moves += [
        (zrows.at[pl.ds(16, 16)], zrows_in.at[0], 1, 0),
        (zrows.at[pl.ds(0, 16)], zrows_in.at[1], -1, 0),
    ]
    last = sends(moves, es_sem, er_sem)
    for copy in last:
        copy.start()

    def fit_lines(b, _):
        for step in range(2):
            at = pl.multiple_of(b * 32 + step * 16, 16)
            both = []
            for part in range(2):
                z = [zmap[n // 6, pl.ds(at + part * 8, 8), (n % 6) * 128 : (n % 6 + 1) * 128] for n in range(12)]
                both.append(joint_of(z))
            g = dot(matrix[...], jnp.concatenate(both, axis=1).astype(BF16))
            g = g[0:128] + g[128:256]
            for k in range(16):
                gbuf[k, pl.ds(at, 8), :] = g[k * 8 : k * 8 + 8, 0:128]
                gbuf[k, pl.ds(at + 8, 8), :] = g[k * 8 : k * 8 + 8, 128:256]
        return 0

    lax.fori_loop(0, LS // 32, fit_lines, 0)
    hbuf[:, 0:8] = jnp.zeros((4, 8, 128), F32)
    hbuf[:, 8 + LS : 16 + LS] = jnp.zeros((4, 8, 128), F32)
    no_lane = jnp.zeros((LS, 128), F32)

    def window(k, slot):
        cells = gbuf[k]
        left, right = beside_lanes(cells, no_lane)
        three = cells + left + right
        hbuf[slot, 8 : 8 + LS] = three
        gbuf[k] = hbuf[slot, 7 : 7 + LS] + three + hbuf[slot, 9 : 9 + LS]

    g_copies = []
    for n in range(4):
        for slot in range(4):
            window(n * 4 + slot, slot)
        g_copies.append(
            pltpu.make_async_copy(gbuf.at[pl.ds(n * 4, 4)], g_ref.at[pl.ds(n * 4, 4)], out_sem.at[n])
        )
        g_copies[-1].start()

    for copy in last:
        copy.wait()

    side = jnp.where(iota((32, 1), 0) < 16, has_right, has_left)
    middle = zcols_in[...] * side
    up, down = zcorners[0] * (side * has_up), zcorners[1] * (side * has_down)
    corners = jnp.where(lax.rem(corner_lane, 2) == 0, up[:, 1:2], down[:, 0:1])
    for n in range(12):
        zv[n, 0:1] = middle[16 + n : 17 + n, 0:128]
        zv[n, 1:2] = middle[16 + n : 17 + n, 128:256]
        zv[n, 2:3] = middle[n : n + 1, 0:128]
        zv[n, 3:4] = middle[n : n + 1, 128:256]
        zv[n, 4:5] = jnp.where(mark_lane < 2, corners[16 + n : 17 + n], corners[n : n + 1])
        zv[n, 5:6] = zrows_in[0, n : n + 1] * has_up
        zv[n, 6:7] = zrows_in[1, n : n + 1] * has_down
        zv[n, 7:8] = jnp.zeros((1, 128), F32)
    g = dot(matrix[...], joint_of([zv[n] for n in range(12)]).astype(BF16))
    g = g[0:128] + g[128:256]
    gv[...] = g
    corner = gv[pl.ds(4, 16, stride=8), :]
    lane16 = iota((16, 128), 1)
    for side_n in range(2):
        edge_line = gv[pl.ds(5 + side_n, 16, stride=8), :]
        left, right = corner[:, side_n : side_n + 1], corner[:, 2 + side_n : 3 + side_n]
        halo_lines[side_n] = (
            edge_line
            + jnp.where(lane16 == 0, left, pltpu.roll(edge_line, 1, 1))
            + jnp.where(lane16 == 127, right, pltpu.roll(edge_line, 127, 1))
        )
    turned = g.T
    columns = jnp.concatenate([turned, pltpu.roll(turned, 127, 1)], axis=0)
    hbuf[0, 8 : 8 + LS] = columns
    turned_ref[...] = halves(hbuf[0, 7 : 7 + LS] + columns + hbuf[0, 9 : 9 + LS])
    pltpu.make_async_copy(payload.at[pl.ds(0, DEVICES - 1)], payload.at[pl.ds(0, DEVICES - 1)], send_sem).wait()
    for copy in g_copies:
        copy.wait()


def finish_kernel(cells_hbm, columns_hbm, lines_hbm, out_hbm, cells, columns, halo_lines, in_sem, small_sem, out_sem):
    small = [
        pltpu.make_async_copy(columns_hbm, columns, small_sem.at[0]),
        pltpu.make_async_copy(lines_hbm, halo_lines, small_sem.at[1]),
    ]
    parts = 16 // FINISH

    def moved(src, dst, sem):
        return [
            pltpu.make_async_copy(src.at[pl.ds(n * FINISH, FINISH)], dst.at[pl.ds(n * FINISH, FINISH)], sem.at[n])
            for n in range(parts)
        ]

    loads, stores = moved(cells_hbm, cells, in_sem), moved(cells, out_hbm, out_sem)
    for copy in small + loads:
        copy.start()
    for copy in small:
        copy.wait()
    qr, qc = lax.rem(iota((256, 128), 0), 128), iota((256, 128), 1)
    for n in range(parts):
        loads[n].wait()
        for k in range(n * FINISH, (n + 1) * FINISH):
            place = jnp.where(((qr == k * 8) & (qc == 0)) | ((qr == k * 8 + 2) & (qc == 127)), 1.0, 0.0).astype(BF16)
            cells[k] = cells[k] + dot(columns[...], place)
            cells[k, 0:1] = cells[k, 0:1] + halo_lines[0, k : k + 1]
            cells[k, LS - 1 : LS] = cells[k, LS - 1 : LS] + halo_lines[1, k : k + 1]
        stores[n].start()
    for copy in stores:
        copy.wait()


def body(radar_l, radar_s, weights_l, weights_s, owner_l, owner_s, slot_l, slot_s, models):
    dma = pltpu.SemaphoreType.DMA
    vmem = pltpu.VMEM
    cells, turned, halo_lines = pl.pallas_call(
        main_kernel,
        out_shape=(
            jax.ShapeDtypeStruct((16, LS, 128), F32),
            jax.ShapeDtypeStruct((256, 256), BF16),
            jax.ShapeDtypeStruct((2, 16, 128), F32),
        ),
        in_specs=[pl.BlockSpec(memory_space=pl.ANY)] * 9,
        out_specs=[pl.BlockSpec(memory_space=pl.ANY)] + [pl.BlockSpec(memory_space=pltpu.VMEM)] * 2,
        scratch_shapes=[
            vmem((6, LL, 128), BF16),
            vmem((6, LS, 128), BF16),
            vmem((1, LL), I32),
            vmem((1, LS), I32),
            vmem((LL,), I32),
            vmem((LS,), I32),
            vmem((16, NJ), F32),
            vmem((TILES, 128, 128), BF16),
            vmem((6, EXT, 128), F32),
            vmem((6, EXT, 128), F32),
            vmem((TILES + 1, 8, 128), F32),
            vmem((256, 128), F32),
            vmem((DEVICES, ROWS, 128), BF16),
            vmem((DEVICES, ROWS, 128), BF16),
            vmem((6, 256, 128), BF16),
            vmem((16, TILES + 128), BF16),
            vmem((2, 16, 128), BF16),
            vmem((2, 16, TILES), BF16),
            vmem((4, 16, 128), BF16),
            vmem((2, 16, 128), BF16),
            vmem((16, DEVICES), I32),
            pltpu.SMEM((16, DEVICES), I32),
            vmem((DEVICES, 128), F32),
            vmem((256, NJ * 8), BF16),
            vmem((2, LS, 768), F32),
            vmem((32, LS + 128), F32),
            vmem((32, 128), F32),
            vmem((32, LS), F32),
            vmem((2, 32, 128), F32),
            vmem((2, 16, 128), F32),
            vmem((12, 8, 128), F32),
            vmem((16, LS, 128), F32),
            vmem((128, 128), F32),
            vmem((4, LS + 16, 128), F32),
            dma((7,)),
            dma((8,)),
            dma((8,)),
            dma((8,)),
            dma,
            dma((DEVICES,)),
            dma((8,)),
            dma((8,)),
            dma,
            dma((4,)),
        ],
        compiler_params=pltpu.CompilerParams(
            collective_id=0, has_side_effects=True, vmem_limit_bytes=60 << 20
        ),
        name="unite",
    )(
        radar_l, radar_s, weights_l, weights_s,
        owner_l.reshape(1, LL), owner_s.reshape(1, LS), slot_l, slot_s, models,
    )
    return pl.pallas_call(
        finish_kernel,
        out_shape=jax.ShapeDtypeStruct((16, LS, 128), F32),
        in_specs=[pl.BlockSpec(memory_space=pl.ANY)] * 3,
        out_specs=pl.BlockSpec(memory_space=pl.ANY),
        scratch_shapes=[
            vmem((16, LS, 128), F32),
            vmem((256, 256), BF16),
            vmem((2, 16, 128), F32),
            dma((16 // FINISH,)),
            dma((2,)),
            dma((16 // FINISH,)),
        ],
        compiler_params=pltpu.CompilerParams(vmem_limit_bytes=60 << 20),
        name="finish",
    )(cells, turned, halo_lines)


def solution(mesh):
    in_specs = (
        P(None, "sec", "swath"),
        P(None, "sec", "swath"),
        P(("sec", "swath"), None, None),
        P(("sec", "swath"), None, None),
        P(("sec", "swath"), None),
        P(("sec", "swath"), None),
        P(("sec", "swath")),
        P(("sec", "swath")),
        P(),
    )
    out_specs = P(None, "sec", "swath")
    return jax.shard_map(body, mesh=mesh, in_specs=in_specs, out_specs=out_specs, check_vma=False)
```
